1024 devices in a mesh: img: 64 (over z, x_lo, core), txt: 16 (over x_hi, y).
Axes of the slice: x: 8 (x_hi: 2, x_lo: 4; x = x_hi * 4 + x_lo), y: 8, z: 8, core: 2. Of those that a mesh axis runs over, the one named last changes fastest.
Arguments:
- image_embed: bfloat16 [8192, 1152], P(('img', 'txt')), may hold values from -8 to 8
- text_embed: bfloat16 [8192, 1152], P(('txt', 'img')), may hold values from -8 to 8
- pair_index: int32 [8192], P(('img', 'txt')), may hold values from 0 to 8191, as said below
- log_scale: float32 [1], replicated, may hold values from 2 to 2.6
- bias: float32 [1], replicated, may hold values from -9 to -6
Outputs:
- image_grad: float32 [8192, 1152], P(('img', 'txt'))
- text_grad: float32 [8192, 1152], P(('txt', 'img'))
- stats: float32 [3], replicated
The draws below stay inside these ranges and needn't reach their ends.
Inputs may be any that keep to these rules, and one draw needn't show every extreme that they name: pair_index is a permutation of the text rows.
All inputs are finite; a program needn't handle non-finite values.
Results may differ from the reference program's by a relative error of at most 0.0026.
Values may be sent and summed in bfloat16 or wider, within the bound.
No kernel may reach another device: no remote copies, remote signals or barrier semaphores. Data moves between devices by JAX's collectives and lax.ppermute only.
A program may use at most 32 MiB of HBM per device.

```python
import math
import jax
import jax.numpy as jnp
from jax import lax

D = 1152
ROWS = 8
BATCH = 8192
N_TXT = 16


def shared_layout(key):
    order = jax.random.permutation(jax.random.fold_in(key, 101), BATCH).astype(jnp.int32)
    clusters = max(BATCH // 48, 2)
    labels = jax.random.randint(jax.random.fold_in(key, 102), (BATCH,), 0, clusters).astype(jnp.int32)
    return (order, labels, clusters)


def image_core(key, center_share):
    order, labels, clusters = shared_layout(key)
    centers = jax.random.normal(jax.random.fold_in(key, 103), (clusters, D), jnp.float32)
    noise = jax.random.normal(jax.random.fold_in(key, 105), (BATCH, D), jnp.float32)
    rest = 1.0 - center_share
    core = math.sqrt(center_share) * centers[labels] + math.sqrt(rest) * noise
    return (core, order)


def draw_pair_index(key, part):
    order, labels, clusters = shared_layout(key)
    return order


def draw_image_embed(key, part):
    core, order = image_core(key, 0.7)
    spread = 0.7
    own_key = jax.random.fold_in(key, 3)
    row_scale = jnp.exp(spread * jax.random.uniform(own_key, (BATCH, 1), jnp.float32, -1.0, 1.0))
    return jnp.clip(core * row_scale, -8.0, 8.0).astype(jnp.bfloat16)


def draw_text_embed(key, part):
    core, order = image_core(key, 0.7)
    spread = 0.7
    agree_low = 0.4
    agree_high = 0.95
    own_key = jax.random.fold_in(key, 5)
    agree = jax.random.uniform(jax.random.fold_in(own_key, 1), (BATCH, 1), jnp.float32, agree_low, agree_high)
    noise = jax.random.normal(jax.random.fold_in(own_key, 2), (BATCH, D), jnp.float32)
    paired = agree * core + jnp.sqrt(1.0 - agree * agree) * noise
    placed = jnp.zeros((BATCH, D), jnp.float32).at[order].set(paired)
    row_scale = jnp.exp(spread * jax.random.uniform(jax.random.fold_in(own_key, 3), (BATCH, 1), jnp.float32, -1.0, 1.0))
    return jnp.clip(placed * row_scale, -8.0, 8.0).astype(jnp.bfloat16)


def setup_inputs(seed: int = 0) -> dict:
    arg_keys = jax.random.split(jax.random.key(seed), 6)
    image_embed = draw_image_embed(jax.random.fold_in(arg_keys[5], 71), 0)
    text_embed = draw_text_embed(jax.random.fold_in(arg_keys[5], 71), 0)
    pair_index = draw_pair_index(jax.random.fold_in(arg_keys[5], 71), 0)
    log_scale = jnp.clip(jax.random.uniform(arg_keys[3], (1,), jnp.float32, 2.0, 2.6), 2.0, 2.6)
    bias = jnp.clip(jax.random.uniform(arg_keys[4], (1,), jnp.float32, -9.0, -6.0), -9.0, -6.0)
    return dict(image_embed=image_embed, text_embed=text_embed, pair_index=pair_index, log_scale=log_scale, bias=bias)


EPS = 1e-06

def normalize(rows):
    values = rows.astype(jnp.float32)
    norm = jnp.sqrt(lax.optimization_barrier(jnp.sum(values * values, axis=1, keepdims=True)) + EPS)
    return (values / norm, norm)

def project(unit, norm, grad):
    return (grad - unit * lax.optimization_barrier(jnp.sum(unit * grad, axis=1, keepdims=True))) / norm

def reference(image_embed, text_embed, pair_index, log_scale, bias):
    scale = jnp.exp(log_scale[0])
    shift = bias[0]
    image_unit, image_norm = normalize(image_embed)
    text_unit, text_norm = normalize(text_embed)
    image_low = image_unit.astype(jnp.bfloat16)
    text_low = text_unit.astype(jnp.bfloat16)
    block = ROWS * N_TXT
    count = BATCH // block
    columns = jnp.arange(BATCH, dtype=jnp.int32)

    def step(carry, index):
        text_total, sums = carry
        start = (index * block).astype(jnp.int32)
        rows = lax.dynamic_slice_in_dim(image_low, start, block, 0)
        pairs = lax.dynamic_slice_in_dim(pair_index, start, block, 0)
        cosine = jnp.dot(rows, text_low.T, preferred_element_type=jnp.float32)
        logits = scale * cosine + shift
        sign = jnp.where(pairs[:, None] == columns[None, :], 1.0, -1.0).astype(logits.dtype)
        dlogit = -sign * jax.nn.sigmoid(-sign * logits)
        dlogit_low = dlogit.astype(jnp.bfloat16)
        image_part = scale * jnp.dot(dlogit_low, text_low, preferred_element_type=jnp.float32)
        text_part = scale * lax.dot_general(dlogit_low, rows, (((0,), (0,)), ((), ())), preferred_element_type=jnp.float32)
        extra = jnp.stack([jnp.sum(jax.nn.softplus(-sign * logits)), jnp.sum(dlogit), jnp.sum(dlogit * scale * cosine)])
        return ((text_total + text_part, sums + extra), image_part)
    init = (jnp.zeros((BATCH, D), jnp.float32), jnp.zeros((3,), jnp.float32))
    (text_total, sums), image_parts = lax.scan(step, init, jnp.arange(count, dtype=jnp.int32))
    image_total = image_parts.reshape(BATCH, D)
    image_grad = project(image_unit, image_norm, image_total)
    text_grad = project(text_unit, text_norm, text_total)
    return (image_grad, text_grad, sums / BATCH)
```

```python
import functools
import jax
import jax.numpy as jnp
from jax import lax
from jax.experimental import pallas as pl
from jax.experimental.pallas import tpu as pltpu
from jax.sharding import Mesh, PartitionSpec as P

EPS = 1e-06
EXTRA = 128
F32 = jnp.float32
BF16 = jnp.bfloat16
VMEM = pl.BlockSpec(memory_space=pltpu.VMEM)
SMEM = pl.BlockSpec(memory_space=pltpu.SMEM)


def unit_and_norm(rows):
    values = rows.astype(F32)
    norm = jnp.sqrt(jnp.sum(values * values, axis=1, keepdims=True) + EPS)
    return values / norm, norm


def lanes(rows):
    return lax.broadcasted_iota(jnp.int32, (rows, EXTRA), 1)


def pack_kernel(image_ref, text_ref, pair_ref, image_out, text_out):
    width = image_ref.shape[1]
    image_low, _ = unit_and_norm(image_ref[...])
    text_low, _ = unit_and_norm(text_ref[...])
    rows = image_ref.shape[0]
    row = lax.broadcasted_iota(jnp.int32, (rows, EXTRA), 0)
    pair = jnp.zeros((rows, EXTRA), jnp.int32)
    for r in range(rows):
        pair = jnp.where(row == r, pair_ref[r], pair)
    lane = lanes(rows)
    high = lax.shift_right_logical(pair, 7)
    low = lax.bitwise_and(pair, 127)
    extra = jnp.where(lane == 0, high, jnp.where(lane == 1, low, 0)).astype(F32)
    image_two = jnp.concatenate([image_low, image_low], axis=0).astype(BF16)
    text_two = jnp.concatenate([text_low, text_low], axis=0).astype(BF16)
    extra_two = jnp.concatenate([extra, extra], axis=0).astype(BF16)
    step = 2 * rows
    for k in range(image_out.shape[0] // step):
        image_out[k * step : (k + 1) * step, :width] = image_two
        image_out[k * step : (k + 1) * step, width:] = extra_two
    for k in range(text_out.shape[0] // step):
        text_out[k * step : (k + 1) * step, :] = text_two


def split_stats(lane, first, values):
    out = jnp.zeros(lane.shape, F32)
    for n, value in enumerate(values):
        high = value.astype(BF16).astype(F32)
        out = jnp.where(lane == first + n, high, out)
        out = jnp.where(lane == first + 3 + n, value - high, out)
    return out


def score_kernel(own_rows, core_size, row_size, mine_ref, other_ref, text_ref, log_scale_ref, bias_ref, text_out, mine_out, other_out):
    text = text_ref[...]
    count, width = text.shape
    scale = jnp.exp(jnp.zeros((8, 128), F32) + log_scale_ref[0])[0:1, 0:1]
    shift = bias_ref[0]
    base = (lax.axis_index("txt") * (row_size * core_size) + lax.axis_index("core")) * own_rows
    column = lax.broadcasted_iota(jnp.int32, (1, count), 1)
    column = base + (column // own_rows) * (own_rows * core_size) + column % own_rows
    column = column.astype(F32)
    text_part = None
    along_text = None
    totals = None
    for source, target in ((mine_ref, mine_out), (other_ref, other_out)):
        image = source[:, :width]
        extra = source[:, width:].astype(F32)
        pair = extra[:, 0:1] * 128.0 + extra[:, 1:2]
        cosine = lax.dot_general(image, text, (((1,), (1,)), ((), ())), preferred_element_type=F32)
        scaled = scale * cosine
        logits = scaled + shift
        match = pair == column
        arg = jnp.where(match, -logits, logits)
        small = jnp.exp(-jnp.abs(arg))
        inverse = 1.0 / (1.0 + small)
        prob = jnp.where(arg >= 0, inverse, small * inverse)
        dlogit = jnp.where(match, -prob, prob)
        loss = jnp.maximum(arg, 0.0) + jnp.log1p(small)
        low = dlogit.astype(BF16)
        product = low.astype(F32) * scaled
        sums = [
            jnp.sum(loss, axis=(0, 1), keepdims=True),
            jnp.sum(dlogit, axis=(0, 1), keepdims=True),
            jnp.sum(dlogit * scaled, axis=(0, 1), keepdims=True),
        ]
        totals = sums if totals is None else [a + b for a, b in zip(totals, sums)]
        along = jnp.sum(product, axis=1, keepdims=True)
        part = scale * jnp.dot(low, text, preferred_element_type=F32)
        target[:, :width] = part - along * image.astype(F32)
        target[:, width:] = jnp.where(lanes(image.shape[0]) == 0, along, 0.0)
        piece = lax.dot_general(low, image, (((0,), (0,)), ((), ())), preferred_element_type=F32)
        text_part = piece if text_part is None else text_part + piece
        sums = jnp.sum(product, axis=0, keepdims=True)
        along_text = sums if along_text is None else along_text + sums
    along_text = jnp.broadcast_to(along_text, (128, count)).T
    along_text = along_text.astype(BF16).astype(F32)
    text_out[:, :width] = (scale * text_part - along_text[:, 0:1] * text.astype(F32)).astype(BF16)
    lane = lanes(count)
    stats = split_stats(lane, 1, [jnp.broadcast_to(t, lane.shape) for t in totals])
    text_out[:, width:] = jnp.where(lane == 0, along_text, stats).astype(BF16)


def merge_stats(extra, rows):
    peers = extra.shape[0] // rows
    total = jnp.sum(extra.reshape(peers, rows, EXTRA), axis=0)
    return [total[0:1, n : n + 1] + total[0:1, n + 3 : n + 4] for n in (1, 2, 3)]


def join_kernel(own_rows, mine_ref, other_ref, text_extra_ref, out_ref):
    total = mine_ref[...] + other_ref[...]
    width = mine_ref.shape[1] - EXTRA
    out_ref[:, :width] = total[:, :width].astype(BF16)
    lane = lanes(mine_ref.shape[0])
    stats = merge_stats(text_extra_ref[...].astype(F32), own_rows)
    stats = split_stats(lane, 1, [jnp.broadcast_to(t, lane.shape) for t in stats])
    out_ref[:, width:] = jnp.where(lane == 0, total[:, width:], stats).astype(BF16)


def finish(parts_ref, embed_ref, grad_out):
    rows, width = embed_ref.shape
    peers = parts_ref.shape[0] // rows
    total = jnp.sum(parts_ref[...].astype(F32).reshape(peers, rows, width + EXTRA), axis=0)
    unit, norm = unit_and_norm(embed_ref[...])
    grad = total[:, :width] + total[:, width : width + 1] * unit.astype(BF16).astype(F32)
    grad_out[...] = (grad - unit * jnp.sum(unit * grad, axis=1, keepdims=True)) / norm


def stats_kernel(own_rows, extra_ref, out_ref):
    stats = merge_stats(extra_ref[...].astype(F32), own_rows)
    lane = lanes(8)
    out = jnp.zeros(lane.shape, F32)
    for n, value in enumerate(stats):
        out = jnp.where(lane == n, value, out)
    out_ref[...] = out


def shape(*dims, dtype=BF16):
    return jax.ShapeDtypeStruct(dims, dtype)


def per_device(image_embed, text_embed, pair_index, log_scale, bias):
    own_rows, width = image_embed.shape
    row_size, core_size, txt_size = (lax.axis_size(a) for a in ("row", "core", "txt"))
    wide = width + EXTRA
    image_count, text_count = txt_size * own_rows, row_size * own_rows
    image_send, text_send = pl.pallas_call(
        pack_kernel,
        out_shape=(shape(image_count, wide), shape(text_count, width)),
        in_specs=[VMEM, VMEM, SMEM],
        out_specs=(VMEM, VMEM),
    )(image_embed, text_embed, pair_index)
    mine = lax.all_to_all(image_send, "txt", 0, 0, tiled=True)
    text = lax.all_to_all(text_send, "row", 0, 0, tiled=True)
    swap = [(0, 1), (1, 0)]
    other = lax.ppermute(mine, "core", swap)
    text_parts, image_own, image_away = pl.pallas_call(
        functools.partial(score_kernel, own_rows, core_size, row_size),
        out_shape=(
            shape(text_count, wide),
            shape(image_count, wide, dtype=F32),
            shape(image_count, wide, dtype=F32),
        ),
        in_specs=[VMEM, VMEM, VMEM, SMEM, SMEM],
        out_specs=(VMEM, VMEM, VMEM),
    )(mine, other, text, log_scale, bias)
    text_back = lax.all_to_all(text_parts, "row", 0, 0, tiled=True)
    image_came = lax.ppermute(image_away, "core", swap)
    last = width // EXTRA
    image_parts = pl.pallas_call(
        functools.partial(join_kernel, own_rows),
        out_shape=shape(image_count, wide),
        grid=(1,),
        in_specs=[
            pl.BlockSpec((image_count, wide), lambda i: (0, 0)),
            pl.BlockSpec((image_count, wide), lambda i: (0, 0)),
            pl.BlockSpec((text_count, EXTRA), lambda i: (0, last)),
        ],
        out_specs=pl.BlockSpec((image_count, wide), lambda i: (0, 0)),
    )(image_own, image_came, text_back)
    image_back = lax.all_to_all(image_parts, "txt", 0, 0, tiled=True)
    text_grad = pl.pallas_call(
        finish, out_shape=shape(own_rows, width, dtype=F32), in_specs=[VMEM, VMEM], out_specs=VMEM
    )(text_back, text_embed)
    sums = pl.pallas_call(
        functools.partial(stats_kernel, own_rows),
        out_shape=shape(8, EXTRA, dtype=F32),
        grid=(1,),
        in_specs=[pl.BlockSpec((image_count, EXTRA), lambda i: (0, last))],
        out_specs=pl.BlockSpec((8, EXTRA), lambda i: (0, 0)),
    )(image_back)
    sums_came = lax.ppermute(sums, "core", swap)
    image_grad = pl.pallas_call(
        finish, out_shape=shape(own_rows, width, dtype=F32), in_specs=[VMEM, VMEM], out_specs=VMEM
    )(image_back, image_embed)
    batch = own_rows * row_size * core_size * txt_size
    stats = (sums + sums_came)[0, :3] / batch
    return (image_grad, text_grad, stats)


def solution(mesh):
    img, txt = mesh.shape["img"], mesh.shape["txt"]
    split = Mesh(mesh.devices.reshape(img // 2, 2, txt), ("row", "core", "txt"))
    image_spec = P(("row", "core", "txt"), None)
    text_spec = P(("txt", "row", "core"), None)
    return jax.shard_map(
        per_device,
        mesh=split,
        in_specs=(image_spec, text_spec, P(("row", "core", "txt")), P(), P()),
        out_specs=(image_spec, text_spec, P()),
        check_vma=False,
    )
```

```python
import functools
import jax
import jax.numpy as jnp
from jax import lax
from jax.experimental import pallas as pl
from jax.experimental.pallas import tpu as pltpu
from jax.sharding import Mesh, PartitionSpec as P

EPS = 1e-06
EXTRA = 128
F32 = jnp.float32
BF16 = jnp.bfloat16
IMAGE_ORDER = ("z", "x1", "x0", "core", "xh", "y")
TEXT_ORDER = ("xh", "y", "z", "x1", "x0", "core")
TEXT_GROUP = ("z", "x1", "xh")
VMEM = pl.BlockSpec(memory_space=pltpu.VMEM)
SMEM = pl.BlockSpec(memory_space=pltpu.SMEM)


def unit_and_norm(rows):
    values = rows.astype(F32)
    norm = jnp.sqrt(jnp.sum(values * values, axis=1, keepdims=True) + EPS)
    return values / norm, norm


def lanes(rows):
    return lax.broadcasted_iota(jnp.int32, (rows, EXTRA), 1)


def pack_kernel(image_ref, text_ref, pair_ref, image_out, text_out, image_unit, image_norm, text_unit, text_norm):
    rows, width = image_ref.shape
    image_unit[...], image_norm[...] = unit_and_norm(image_ref[...])
    text_unit[...], text_norm[...] = unit_and_norm(text_ref[...])
    row = lax.broadcasted_iota(jnp.int32, (rows, EXTRA), 0)
    pair = jnp.zeros((rows, EXTRA), jnp.int32)
    for r in range(rows):
        pair = jnp.where(row == r, pair_ref[r], pair)
    lane = lanes(rows)
    high = lax.shift_right_logical(pair, 7)
    low = lax.bitwise_and(pair, 127)
    extra = jnp.where(lane == 0, high, jnp.where(lane == 1, low, 0)).astype(F32)
    image_two = jnp.concatenate([image_unit[...]] * 2, axis=0).astype(BF16)
    text_two = jnp.concatenate([text_unit[...]] * 2, axis=0).astype(BF16)
    extra_two = jnp.concatenate([extra] * 2, axis=0).astype(BF16)
    step = 2 * rows
    for k in range(image_out.shape[0] // step):
        image_out[k * step : (k + 1) * step, :width] = image_two
        image_out[k * step : (k + 1) * step, width:] = extra_two
    for k in range(text_out.shape[0] // step):
        text_out[k * step : (k + 1) * step, :] = text_two


def split_stats(lane, first, values):
    out = jnp.zeros(lane.shape, F32)
    for n, value in enumerate(values):
        high = value.astype(BF16).astype(F32)
        out = jnp.where(lane == first + n, high, out)
        out = jnp.where(lane == first + 3 + n, value - high, out)
    return out


def text_columns(own_rows, sizes, count):
    place = lax.broadcasted_iota(jnp.int32, (1, count), 1)
    peer, row = place // own_rows, place % own_rows
    index = {a: lax.axis_index(a) for a in ("x0", "core", "y")}
    index["xh"] = peer % sizes["xh"]
    index["x1"] = (peer // sizes["xh"]) % sizes["x1"]
    index["z"] = peer // (sizes["xh"] * sizes["x1"])
    owner = 0
    for a in TEXT_ORDER:
        owner = owner * sizes[a] + index[a]
    return owner * own_rows + row


def score_kernel(own_rows, sizes, piece_refs, text_ref, log_scale_ref, bias_ref, text_out, stay_out, away_out):
    text = text_ref[...]
    count, width = text.shape
    scale = jnp.exp(jnp.zeros((8, 128), F32) + log_scale_ref[0])[0:1, 0:1]
    column = text_columns(own_rows, sizes, count).astype(F32)
    image = jnp.concatenate([r[:, :width] for r in piece_refs], axis=0)
    extra = jnp.concatenate([r[:, width:] for r in piece_refs], axis=0).astype(F32)
    pair = extra[:, 0:1] * 128.0 + extra[:, 1:2]
    cosine = lax.dot_general(image, text, (((1,), (1,)), ((), ())), preferred_element_type=F32)
    scaled = scale * cosine
    logits = scaled + bias_ref[0]
    match = pair == column
    arg = jnp.where(match, -logits, logits)
    small = jnp.exp(-jnp.abs(arg))
    inverse = 1.0 / (1.0 + small)
    prob = jnp.where(arg >= 0, inverse, small * inverse)
    dlogit = jnp.where(match, -prob, prob)
    loss = jnp.maximum(arg, 0.0) + jnp.log1p(small)
    low = dlogit.astype(BF16)
    product = low.astype(F32) * scaled
    totals = [jnp.sum(v, axis=(0, 1), keepdims=True) for v in (loss, dlogit, dlogit * scaled)]
    along_image = jnp.sum(product, axis=1, keepdims=True)
    along_text = jnp.broadcast_to(jnp.sum(product, axis=0, keepdims=True), (128, count)).T
    along_text = along_text.astype(BF16).astype(F32)
    low_turned = dlogit.T.astype(BF16)
    half = image.shape[0] // 2
    block = width // 3
    for first in range(0, width, block):
        cols = slice(first, first + block)
        part = scale * jnp.dot(low, text[:, cols], preferred_element_type=F32)
        part = part - along_image * image[:, cols].astype(F32)
        stay_out[:, cols] = part[:half]
        away_out[:, cols] = part[half:]
        part = scale * jnp.dot(low_turned, image[:, cols], preferred_element_type=F32)
        text_out[:, cols] = (part - along_text[:, 0:1] * text[:, cols].astype(F32)).astype(BF16)
    kept = jnp.where(lanes(2 * half) == 0, along_image, 0.0)
    stay_out[:, width:] = kept[:half]
    away_out[:, width:] = kept[half:]
    lane = lanes(count)
    stats = split_stats(lane, 1, [jnp.broadcast_to(t, lane.shape) for t in totals])
    text_out[:, width:] = jnp.where(lane == 0, along_text, stats).astype(BF16)


def merge_stats(extra, rows):
    peers = extra.shape[0] // rows
    total = jnp.sum(extra.reshape(peers, rows, EXTRA), axis=0)
    return [total[0:1, n : n + 1] + total[0:1, n + 3 : n + 4] for n in (1, 2, 3)]


def add_kernel(stay_ref, came_ref, keep_out, send_out):
    half = keep_out.shape[0]
    keep_out[...] = stay_ref[:half, :] + came_ref[:half, :]
    send_out[...] = stay_ref[half:, :] + came_ref[half:, :]


def join_kernel(own_rows, keep_ref, came_ref, text_back_ref, out_ref):
    width = keep_ref.shape[1] - EXTRA
    out_ref[:, :width] = (keep_ref[:, :width] + came_ref[:, :width]).astype(BF16)
    lane = lanes(keep_ref.shape[0])
    stats = merge_stats(text_back_ref[:, width:].astype(F32), own_rows)
    stats = split_stats(lane, 1, [jnp.broadcast_to(t, lane.shape) for t in stats])
    along = keep_ref[:, width:] + came_ref[:, width:]
    out_ref[:, width:] = jnp.where(lane == 0, along, stats).astype(BF16)


def finish_kernel(parts_ref, unit_ref, norm_ref, grad_out):
    rows, width = unit_ref.shape
    peers = parts_ref.shape[0] // rows
    total = jnp.sum(parts_ref[...].astype(F32).reshape(peers, rows, width + EXTRA), axis=0)
    unit = unit_ref[...]
    grad = total[:, :width] + total[:, width : width + 1] * unit.astype(BF16).astype(F32)
    grad_out[...] = (grad - unit * jnp.sum(unit * grad, axis=1, keepdims=True)) / norm_ref[...]


def stats_kernel(own_rows, parts_ref, out_ref):
    width = parts_ref.shape[1] - EXTRA
    lane = lanes(8)
    out = jnp.zeros(lane.shape, F32)
    for n, value in enumerate(merge_stats(parts_ref[:, width:].astype(F32), own_rows)):
        out = jnp.where(lane == n, value, out)
    out_ref[...] = jnp.broadcast_to(out[None], out_ref.shape)


def shape(*dims, dtype=BF16):
    return jax.ShapeDtypeStruct(dims, dtype)


def call(kernel, outs, *args, scalars=0, flops=0):
    size = sum(a.size * a.dtype.itemsize for a in args)
    return pl.pallas_call(
        kernel,
        out_shape=outs,
        in_specs=[VMEM] * (len(args) - scalars) + [SMEM] * scalars,
        out_specs=jax.tree.map(lambda _: VMEM, outs),
        cost_estimate=pl.CostEstimate(flops=flops, bytes_accessed=4 * size, transcendentals=0),
        compiler_params=pltpu.CompilerParams(vmem_limit_bytes=40 * 1024 * 1024),
    )(*args)


def per_device(image_embed, text_embed, pair_index, log_scale, bias):
    own_rows, width = image_embed.shape
    sizes = {a: lax.axis_size(a) for a in IMAGE_ORDER}
    wide = width + EXTRA
    row_count = sizes["y"] * own_rows
    text_count = own_rows
    for a in TEXT_GROUP:
        text_count *= sizes[a]
    unit_shape, norm_shape = shape(own_rows, width, dtype=F32), shape(own_rows, 1, dtype=F32)
    image_send, text_send, image_unit, image_norm, text_unit, text_norm = call(
        pack_kernel,
        (shape(row_count, wide), shape(text_count, width), unit_shape, norm_shape, unit_shape, norm_shape),
        image_embed, text_embed, pair_index, scalars=1,
    )
    swap = [(0, 1), (1, 0)]
    piece = lax.all_to_all(image_send, "y", 0, 0, tiled=True)
    text = lax.all_to_all(text_send, TEXT_GROUP, 0, 0, tiled=True)
    piece_x = lax.ppermute(piece, "x0", swap)
    piece_core = lax.ppermute(piece, "core", swap)
    piece_both = lax.ppermute(piece_x, "core", swap)

    def score(a, b, c, d, text_ref, *rest):
        score_kernel(own_rows, sizes, (a, b, c, d), text_ref, *rest)

    text_parts, stay, away = call(
        score,
        (shape(text_count, wide), shape(2 * row_count, wide, dtype=F32), shape(2 * row_count, wide, dtype=F32)),
        piece, piece_x, piece_core, piece_both, text, log_scale, bias,
        scalars=2, flops=3 * 2 * 4 * row_count * text_count * width,
    )
    text_back = lax.all_to_all(text_parts, TEXT_GROUP, 0, 0, tiled=True)
    came = lax.ppermute(away, "core", swap)
    quarter = shape(row_count, wide, dtype=F32)
    keep, send = call(add_kernel, (quarter, quarter), stay, came)
    came_x = lax.ppermute(send, "x0", swap)
    image_parts = call(
        functools.partial(join_kernel, own_rows), shape(row_count, wide), keep, came_x, text_back
    )
    image_back = lax.all_to_all(image_parts, "y", 0, 0, tiled=True)
    text_grad = call(finish_kernel, unit_shape, text_back, text_unit, text_norm)
    four = sizes["x0"] * sizes["core"]
    sums = call(functools.partial(stats_kernel, own_rows), shape(four, 8, EXTRA, dtype=F32), image_back)
    sums = lax.all_to_all(sums, ("x0", "core"), 0, 0, tiled=True)
    image_grad = call(finish_kernel, unit_shape, image_back, image_unit, image_norm)
    batch = own_rows
    for a in IMAGE_ORDER:
        batch *= sizes[a]
    stats = jnp.sum(sums[:, 0, :3], axis=0) / batch
    return (image_grad, text_grad, stats)


def solution(mesh):
    img, txt = mesh.shape["img"], mesh.shape["txt"]
    parts = (img // 8, 2, 2, 2, 2, txt // 2)
    split = Mesh(mesh.devices.reshape(parts), IMAGE_ORDER)
    image_spec, text_spec = P(IMAGE_ORDER, None), P(TEXT_ORDER, None)
    return jax.shard_map(
        per_device,
        mesh=split,
        in_specs=(image_spec, text_spec, P(IMAGE_ORDER), P(), P()),
        out_specs=(image_spec, text_spec, P()),
        check_vma=False,
    )
```

```python
import functools
import math
import jax
import jax.numpy as jnp
from jax import lax
from jax.experimental import pallas as pl
from jax.experimental.pallas import tpu as pltpu
from jax.sharding import Mesh, PartitionSpec as P

EPS = 1e-06
EXTRA = 128
F32 = jnp.float32
BF16 = jnp.bfloat16
IMAGE_ORDER = ("z", "x1", "x0", "core", "xh", "yh", "y0")
TEXT_ORDER = ("xh", "yh", "y0", "z", "x1", "x0", "core")
TEXT_GROUP = ("z", "x1", "xh")
IMAGE_GROUP = ("x0", "yh")
PAIR = "y0"
VMEM = pl.BlockSpec(memory_space=pltpu.VMEM)
SMEM = pl.BlockSpec(memory_space=pltpu.SMEM)


def unit_and_norm(rows):
    values = rows.astype(F32)
    norm = jnp.sqrt(jnp.sum(values * values, axis=1, keepdims=True) + EPS)
    return values / norm, norm


def lanes(rows):
    return lax.broadcasted_iota(jnp.int32, (rows, EXTRA), 1)


def pack_kernel(image_ref, text_ref, pair_ref, image_out, text_out, image_unit, image_norm, text_unit, text_norm):
    rows, width = image_ref.shape
    image_unit[...], image_norm[...] = unit_and_norm(image_ref[...])
    text_unit[...], text_norm[...] = unit_and_norm(text_ref[...])
    row = lax.broadcasted_iota(jnp.int32, (rows, EXTRA), 0)
    pair = jnp.zeros((rows, EXTRA), jnp.int32)
    for r in range(rows):
        pair = jnp.where(row == r, pair_ref[r], pair)
    lane = lanes(rows)
    high = lax.shift_right_logical(pair, 7)
    low = lax.bitwise_and(pair, 127)
    extra = jnp.where(lane == 0, high, jnp.where(lane == 1, low, 0)).astype(F32)
    image_two = jnp.concatenate([image_unit[...]] * 2, axis=0).astype(BF16)
    text_two = jnp.concatenate([text_unit[...]] * 2, axis=0).astype(BF16)
    extra_two = jnp.concatenate([extra] * 2, axis=0).astype(BF16)
    step = 2 * rows
    for k in range(image_out.shape[0] // step):
        image_out[k * step : (k + 1) * step, :width] = image_two
        image_out[k * step : (k + 1) * step, width:] = extra_two
    for k in range(text_out.shape[0] // step):
        text_out[k * step : (k + 1) * step, :] = text_two


def split_stats(lane, first, values):
    out = jnp.zeros(lane.shape, F32)
    for n, value in enumerate(values):
        high = value.astype(BF16).astype(F32)
        out = jnp.where(lane == first + n, high, out)
        out = jnp.where(lane == first + 3 + n, value - high, out)
    return out


def text_columns(own_rows, sizes, count):
    place = lax.broadcasted_iota(jnp.int32, (1, count), 1)
    peer, row = place // own_rows, place % own_rows
    index = {a: lax.axis_index(a) for a in IMAGE_GROUP + (PAIR, "core")}
    for a in reversed(TEXT_GROUP):
        index[a] = peer % sizes[a]
        peer = peer // sizes[a]
    owner = 0
    for a in TEXT_ORDER:
        owner = owner * sizes[a] + index[a]
    return owner * own_rows + row


def score_kernel(own_rows, sizes, piece_refs, text_ref, log_scale_ref, bias_ref, text_out, stay_out, away_out):
    text = text_ref[...]
    count, width = text.shape
    scale = jnp.exp(jnp.zeros((8, 128), F32) + log_scale_ref[0])[0:1, 0:1]
    column = text_columns(own_rows, sizes, count).astype(F32)
    image = jnp.concatenate([r[:, :width] for r in piece_refs], axis=0)
    extra = jnp.concatenate([r[:, width:] for r in piece_refs], axis=0).astype(F32)
    pair = extra[:, 0:1] * 128.0 + extra[:, 1:2]
    cosine = lax.dot_general(image, text, (((1,), (1,)), ((), ())), preferred_element_type=F32)
    scaled = scale * cosine
    logits = scaled + bias_ref[0]
    match = pair == column
    arg = jnp.where(match, -logits, logits)
    small = jnp.exp(-jnp.abs(arg))
    inverse = 1.0 / (1.0 + small)
    prob = jnp.where(arg >= 0, inverse, small * inverse)
    dlogit = jnp.where(match, -prob, prob)
    loss = jnp.maximum(arg, 0.0) + jnp.log1p(small)
    low = dlogit.astype(BF16)
    product = low.astype(F32) * scaled
    totals = [jnp.sum(v, axis=(0, 1), keepdims=True) for v in (loss, dlogit, dlogit * scaled)]
    along_image = jnp.sum(product, axis=1, keepdims=True)
    along_text = jnp.broadcast_to(jnp.sum(product, axis=0, keepdims=True), (128, count)).T
    along_text = along_text.astype(BF16).astype(F32)
    low_turned = dlogit.T.astype(BF16)
    half = image.shape[0] // 2
    block = width // 3
    for first in range(0, width, block):
        cols = slice(first, first + block)
        part = scale * jnp.dot(low, text[:, cols], preferred_element_type=F32)
        part = part - along_image * image[:, cols].astype(F32)
        stay_out[:, cols] = part[:half]
        away_out[:, cols] = part[half:]
        part = scale * jnp.dot(low_turned, image[:, cols], preferred_element_type=F32)
        text_out[:, cols] = (part - along_text[:, 0:1] * text[:, cols].astype(F32)).astype(BF16)
    kept = jnp.where(lanes(2 * half) == 0, along_image, 0.0)
    stay_out[:, width:] = kept[:half]
    away_out[:, width:] = kept[half:]
    lane = lanes(count)
    stats = split_stats(lane, 1, [jnp.broadcast_to(t, lane.shape) for t in totals])
    text_out[:, width:] = jnp.where(lane == 0, along_text, stats).astype(BF16)


def merge_stats(extra, rows):
    peers = extra.shape[0] // rows
    total = jnp.sum(extra.reshape(peers, rows, EXTRA), axis=0)
    return [total[0:1, n : n + 1] + total[0:1, n + 3 : n + 4] for n in (1, 2, 3)]


def add_kernel(stay_ref, came_ref, keep_out, send_out):
    half = keep_out.shape[0]
    keep_out[...] = stay_ref[:half, :] + came_ref[:half, :]
    send_out[...] = stay_ref[half:, :] + came_ref[half:, :]


def join_kernel(own_rows, keep_ref, came_ref, text_back_ref, out_ref):
    width = keep_ref.shape[1] - EXTRA
    out_ref[:, :width] = (keep_ref[:, :width] + came_ref[:, :width]).astype(BF16)
    lane = lanes(keep_ref.shape[0])
    stats = merge_stats(text_back_ref[:, width:].astype(F32), own_rows)
    stats = split_stats(lane, 1, [jnp.broadcast_to(t, lane.shape) for t in stats])
    along = keep_ref[:, width:] + came_ref[:, width:]
    out_ref[:, width:] = jnp.where(lane == 0, along, stats).astype(BF16)


def finish_kernel(parts_ref, unit_ref, norm_ref, grad_out):
    rows, width = unit_ref.shape
    peers = parts_ref.shape[0] // rows
    total = jnp.sum(parts_ref[...].astype(F32).reshape(peers, rows, width + EXTRA), axis=0)
    unit = unit_ref[...]
    grad = total[:, :width] + total[:, width : width + 1] * unit.astype(BF16).astype(F32)
    grad_out[...] = (grad - unit * jnp.sum(unit * grad, axis=1, keepdims=True)) / norm_ref[...]


def stats_kernel(own_rows, parts_ref, out_ref):
    width = parts_ref.shape[1] - EXTRA
    lane = lanes(8)
    out = jnp.zeros(lane.shape, F32)
    for n, value in enumerate(merge_stats(parts_ref[:, width:].astype(F32), own_rows)):
        out = jnp.where(lane == n, value, out)
    out_ref[...] = jnp.broadcast_to(out[None], out_ref.shape)


def shape(*dims, dtype=BF16):
    return jax.ShapeDtypeStruct(dims, dtype)


def call(kernel, outs, *args, scalars=0, flops=0, limit=40 * 1024 * 1024):
    size = sum(a.size * a.dtype.itemsize for a in args)
    return pl.pallas_call(
        kernel,
        out_shape=outs,
        in_specs=[VMEM] * (len(args) - scalars) + [SMEM] * scalars,
        out_specs=jax.tree.map(lambda _: VMEM, outs),
        cost_estimate=pl.CostEstimate(flops=flops, bytes_accessed=4 * size, transcendentals=0),
        compiler_params=pltpu.CompilerParams(vmem_limit_bytes=limit),
    )(*args)


def per_device(image_embed, text_embed, pair_index, log_scale, bias):
    own_rows, width = image_embed.shape
    sizes = {a: lax.axis_size(a) for a in IMAGE_ORDER}
    wide = width + EXTRA
    row_count = math.prod(sizes[a] for a in IMAGE_GROUP) * own_rows
    text_count = math.prod(sizes[a] for a in TEXT_GROUP) * own_rows
    unit_shape, norm_shape = shape(own_rows, width, dtype=F32), shape(own_rows, 1, dtype=F32)
    image_send, text_send, image_unit, image_norm, text_unit, text_norm = call(
        pack_kernel,
        (shape(row_count, wide), shape(text_count, width), unit_shape, norm_shape, unit_shape, norm_shape),
        image_embed, text_embed, pair_index, scalars=1, limit=None,
    )
    swap = [(0, 1), (1, 0)]
    piece = lax.all_to_all(image_send, IMAGE_GROUP, 0, 0, tiled=True)
    text = lax.all_to_all(text_send, TEXT_GROUP, 0, 0, tiled=True)
    piece_pair = lax.ppermute(piece, PAIR, swap)
    piece_core = lax.ppermute(piece, "core", swap)
    piece_both = lax.ppermute(piece_pair, "core", swap)

    def score(a, b, c, d, text_ref, *rest):
        score_kernel(own_rows, sizes, (a, b, c, d), text_ref, *rest)

    text_parts, stay, away = call(
        score,
        (shape(text_count, wide), shape(2 * row_count, wide, dtype=F32), shape(2 * row_count, wide, dtype=F32)),
        piece, piece_pair, piece_core, piece_both, text, log_scale, bias,
        scalars=2, flops=3 * 2 * 4 * row_count * text_count * width,
    )
    text_back = lax.all_to_all(text_parts, TEXT_GROUP, 0, 0, tiled=True)
    came = lax.ppermute(away, "core", swap)
    quarter = shape(row_count, wide, dtype=F32)
    keep, send = call(add_kernel, (quarter, quarter), stay, came)
    came_pair = lax.ppermute(send, PAIR, swap)
    image_parts = call(
        functools.partial(join_kernel, own_rows), shape(row_count, wide), keep, came_pair, text_back
    )
    image_back = lax.all_to_all(image_parts, IMAGE_GROUP, 0, 0, tiled=True)
    text_grad = call(finish_kernel, unit_shape, text_back, text_unit, text_norm)
    four = sizes[PAIR] * sizes["core"]
    sums = call(functools.partial(stats_kernel, own_rows), shape(four, 8, EXTRA, dtype=F32), image_back)
    sums = lax.all_to_all(sums, (PAIR, "core"), 0, 0, tiled=True)
    image_grad = call(finish_kernel, unit_shape, image_back, image_unit, image_norm)
    batch = own_rows * math.prod(sizes.values())
    stats = jnp.sum(sums[:, 0, :3], axis=0) / batch
    return (image_grad, text_grad, stats)


def solution(mesh):
    img, txt = mesh.shape["img"], mesh.shape["txt"]
    parts = (img // 8, 2, 2, 2, 2, txt // 4, 2)
    split = Mesh(mesh.devices.reshape(parts), IMAGE_ORDER)
    image_spec, text_spec = P(IMAGE_ORDER, None), P(TEXT_ORDER, None)
    return jax.shard_map(
        per_device,
        mesh=split,
        in_specs=(image_spec, text_spec, P(IMAGE_ORDER), P(), P()),
        out_specs=(image_spec, text_spec, P()),
        check_vma=False,
    )
```

```python
import functools
import math
import jax
import jax.numpy as jnp
from jax import lax
from jax.experimental import pallas as pl
from jax.experimental.pallas import tpu as pltpu
from jax.sharding import Mesh, PartitionSpec as P

EPS = 1e-06
EXTRA = 128
F32 = jnp.float32
BF16 = jnp.bfloat16
IMAGE_ORDER = ("zh", "z0", "xl", "core", "xh", "yh", "y0")
TEXT_ORDER = ("xh", "yh", "y0", "zh", "z0", "xl", "core")
TEXT_GROUP = ("xh", "xl", "yh")
IMAGE_GROUP = ("zh", "y0")
PAIR = "z0"
VMEM = pl.BlockSpec(memory_space=pltpu.VMEM)
SMEM = pl.BlockSpec(memory_space=pltpu.SMEM)


def unit_and_norm(rows):
    values = rows.astype(F32)
    norm = jnp.sqrt(jnp.sum(values * values, axis=1, keepdims=True) + EPS)
    return values / norm, norm


def lanes(rows):
    return lax.broadcasted_iota(jnp.int32, (rows, EXTRA), 1)


def pack_kernel(image_ref, text_ref, pair_ref, image_out, text_out, image_unit, image_norm, text_unit, text_norm):
    rows, width = image_ref.shape
    image_unit[...], image_norm[...] = unit_and_norm(image_ref[...])
    text_unit[...], text_norm[...] = unit_and_norm(text_ref[...])
    row = lax.broadcasted_iota(jnp.int32, (rows, EXTRA), 0)
    pair = jnp.zeros((rows, EXTRA), jnp.int32)
    for r in range(rows):
        pair = jnp.where(row == r, pair_ref[r], pair)
    lane = lanes(rows)
    high = lax.shift_right_logical(pair, 7)
    low = lax.bitwise_and(pair, 127)
    extra = jnp.where(lane == 0, high, jnp.where(lane == 1, low, 0)).astype(F32)
    image_two = jnp.concatenate([image_unit[...]] * 2, axis=0).astype(BF16)
    text_two = jnp.concatenate([text_unit[...]] * 2, axis=0).astype(BF16)
    extra_two = jnp.concatenate([extra] * 2, axis=0).astype(BF16)
    step = 2 * rows
    for k in range(image_out.shape[0] // step):
        image_out[k * step : (k + 1) * step, :width] = image_two
        image_out[k * step : (k + 1) * step, width:] = extra_two
    for k in range(text_out.shape[0] // step):
        text_out[k * step : (k + 1) * step, :] = text_two


def split_stats(lane, first, values):
    out = jnp.zeros(lane.shape, F32)
    for n, value in enumerate(values):
        high = value.astype(BF16).astype(F32)
        out = jnp.where(lane == first + n, high, out)
        out = jnp.where(lane == first + 3 + n, value - high, out)
    return out


def text_columns(own_rows, sizes, count):
    place = lax.broadcasted_iota(jnp.int32, (1, count), 1)
    peer, row = place // own_rows, place % own_rows
    index = {a: lax.axis_index(a) for a in IMAGE_GROUP + (PAIR, "core")}
    for a in reversed(TEXT_GROUP):
        index[a] = peer % sizes[a]
        peer = peer // sizes[a]
    owner = 0
    for a in TEXT_ORDER:
        owner = owner * sizes[a] + index[a]
    return owner * own_rows + row


def score_kernel(own_rows, sizes, piece_refs, text_ref, log_scale_ref, bias_ref, text_out, stay_out, away_out):
    text = text_ref[...]
    count, width = text.shape
    scale = jnp.exp(jnp.zeros((8, 128), F32) + log_scale_ref[0])[0:1, 0:1]
    column = text_columns(own_rows, sizes, count).astype(F32)
    image = jnp.concatenate([r[:, :width] for r in piece_refs], axis=0)
    extra = jnp.concatenate([r[:, width:] for r in piece_refs], axis=0).astype(F32)
    pair = extra[:, 0:1] * 128.0 + extra[:, 1:2]
    cosine = lax.dot_general(image, text, (((1,), (1,)), ((), ())), preferred_element_type=F32)
    scaled = scale * cosine
    logits = scaled + bias_ref[0]
    match = pair == column
    arg = jnp.where(match, -logits, logits)
    small = jnp.exp(-jnp.abs(arg))
    inverse = 1.0 / (1.0 + small)
    prob = jnp.where(arg >= 0, inverse, small * inverse)
    dlogit = jnp.where(match, -prob, prob)
    loss = jnp.maximum(arg, 0.0) + jnp.log1p(small)
    low = dlogit.astype(BF16)
    product = low.astype(F32) * scaled
    totals = [jnp.sum(v, axis=(0, 1), keepdims=True) for v in (loss, dlogit, dlogit * scaled)]
    along_image = jnp.sum(product, axis=1, keepdims=True)
    along_text = jnp.broadcast_to(jnp.sum(product, axis=0, keepdims=True), (128, count)).T
    along_text = along_text.astype(BF16).astype(F32)
    low_turned = dlogit.T.astype(BF16)
    half = image.shape[0] // 2
    block = width // 3
    for first in range(0, width, block):
        cols = slice(first, first + block)
        part = scale * jnp.dot(low, text[:, cols], preferred_element_type=F32)
        part = part - along_image * image[:, cols].astype(F32)
        stay_out[:, cols] = part[:half]
        away_out[:, cols] = part[half:]
        part = scale * jnp.dot(low_turned, image[:, cols], preferred_element_type=F32)
        text_out[:, cols] = (part - along_text[:, 0:1] * text[:, cols].astype(F32)).astype(BF16)
    kept = jnp.where(lanes(2 * half) == 0, along_image, 0.0)
    stay_out[:, width:] = kept[:half]
    away_out[:, width:] = kept[half:]
    lane = lanes(count)
    stats = split_stats(lane, 1, [jnp.broadcast_to(t, lane.shape) for t in totals])
    text_out[:, width:] = jnp.where(lane == 0, along_text, stats).astype(BF16)


def merge_stats(extra, rows):
    peers = extra.shape[0] // rows
    total = jnp.sum(extra.reshape(peers, rows, EXTRA), axis=0)
    return [total[0:1, n : n + 1] + total[0:1, n + 3 : n + 4] for n in (1, 2, 3)]


def add_kernel(stay_ref, came_ref, keep_out, send_out):
    half = keep_out.shape[0]
    keep_out[...] = stay_ref[:half, :] + came_ref[:half, :]
    send_out[...] = stay_ref[half:, :] + came_ref[half:, :]


def join_kernel(own_rows, keep_ref, came_ref, text_back_ref, out_ref):
    width = keep_ref.shape[1] - EXTRA
    out_ref[:, :width] = (keep_ref[:, :width] + came_ref[:, :width]).astype(BF16)
    lane = lanes(keep_ref.shape[0])
    stats = merge_stats(text_back_ref[:, width:].astype(F32), own_rows)
    stats = split_stats(lane, 1, [jnp.broadcast_to(t, lane.shape) for t in stats])
    along = keep_ref[:, width:] + came_ref[:, width:]
    out_ref[:, width:] = jnp.where(lane == 0, along, stats).astype(BF16)


def finish_kernel(parts_ref, unit_ref, norm_ref, grad_out):
    rows, width = unit_ref.shape
    peers = parts_ref.shape[0] // rows
    total = jnp.sum(parts_ref[...].astype(F32).reshape(peers, rows, width + EXTRA), axis=0)
    unit = unit_ref[...]
    grad = total[:, :width] + total[:, width : width + 1] * unit.astype(BF16).astype(F32)
    grad_out[...] = (grad - unit * jnp.sum(unit * grad, axis=1, keepdims=True)) / norm_ref[...]


def stats_kernel(own_rows, parts_ref, out_ref):
    width = parts_ref.shape[1] - EXTRA
    lane = lanes(8)
    out = jnp.zeros(lane.shape, F32)
    for n, value in enumerate(merge_stats(parts_ref[:, width:].astype(F32), own_rows)):
        out = jnp.where(lane == n, value, out)
    out_ref[...] = jnp.broadcast_to(out[None], out_ref.shape)


def shape(*dims, dtype=BF16):
    return jax.ShapeDtypeStruct(dims, dtype)


def call(kernel, outs, *args, scalars=0, flops=0, limit=40 * 1024 * 1024):
    size = sum(a.size * a.dtype.itemsize for a in args)
    return pl.pallas_call(
        kernel,
        out_shape=outs,
        in_specs=[VMEM] * (len(args) - scalars) + [SMEM] * scalars,
        out_specs=jax.tree.map(lambda _: VMEM, outs),
        cost_estimate=pl.CostEstimate(flops=flops, bytes_accessed=4 * size, transcendentals=0),
        compiler_params=pltpu.CompilerParams(vmem_limit_bytes=limit),
    )(*args)


def per_device(image_embed, text_embed, pair_index, log_scale, bias):
    own_rows, width = image_embed.shape
    sizes = {a: lax.axis_size(a) for a in IMAGE_ORDER}
    wide = width + EXTRA
    row_count = math.prod(sizes[a] for a in IMAGE_GROUP) * own_rows
    text_count = math.prod(sizes[a] for a in TEXT_GROUP) * own_rows
    unit_shape, norm_shape = shape(own_rows, width, dtype=F32), shape(own_rows, 1, dtype=F32)
    image_send, text_send, image_unit, image_norm, text_unit, text_norm = call(
        pack_kernel,
        (shape(row_count, wide), shape(text_count, width), unit_shape, norm_shape, unit_shape, norm_shape),
        image_embed, text_embed, pair_index, scalars=1, limit=None,
    )
    swap = [(0, 1), (1, 0)]
    piece = lax.all_to_all(image_send, IMAGE_GROUP, 0, 0, tiled=True)
    text = lax.all_to_all(text_send, TEXT_GROUP, 0, 0, tiled=True)
    piece_pair = lax.ppermute(piece, PAIR, swap)
    piece_core = lax.ppermute(piece, "core", swap)
    piece_both = lax.ppermute(piece_pair, "core", swap)

    def score(a, b, c, d, text_ref, *rest):
        score_kernel(own_rows, sizes, (a, b, c, d), text_ref, *rest)

    text_parts, stay, away = call(
        score,
        (shape(text_count, wide), shape(2 * row_count, wide, dtype=F32), shape(2 * row_count, wide, dtype=F32)),
        piece, piece_pair, piece_core, piece_both, text, log_scale, bias,
        scalars=2, flops=3 * 2 * 4 * row_count * text_count * width,
    )
    text_back = lax.all_to_all(text_parts, TEXT_GROUP, 0, 0, tiled=True)
    came = lax.ppermute(away, "core", swap)
    quarter = shape(row_count, wide, dtype=F32)
    keep, send = call(add_kernel, (quarter, quarter), stay, came)
    came_pair = lax.ppermute(send, PAIR, swap)
    image_parts = call(
        functools.partial(join_kernel, own_rows), shape(row_count, wide), keep, came_pair, text_back
    )
    image_back = lax.all_to_all(image_parts, IMAGE_GROUP, 0, 0, tiled=True)
    text_grad = call(finish_kernel, unit_shape, text_back, text_unit, text_norm)
    four = sizes[PAIR] * sizes["core"]
    sums = call(functools.partial(stats_kernel, own_rows), shape(four, 8, EXTRA, dtype=F32), image_back)
    sums = lax.all_to_all(sums, (PAIR, "core"), 0, 0, tiled=True)
    image_grad = call(finish_kernel, unit_shape, image_back, image_unit, image_norm)
    batch = own_rows * math.prod(sizes.values())
    stats = jnp.sum(sums[:, 0, :3], axis=0) / batch
    return (image_grad, text_grad, stats)


def solution(mesh):
    img, txt = mesh.shape["img"], mesh.shape["txt"]
    parts = (img // 16, 2, 4, 2, 2, txt // 4, 2)
    split = Mesh(mesh.devices.reshape(parts), IMAGE_ORDER)
    image_spec, text_spec = P(IMAGE_ORDER, None), P(TEXT_ORDER, None)
    return jax.shard_map(
        per_device,
        mesh=split,
        in_specs=(image_spec, text_spec, P(IMAGE_ORDER), P(), P()),
        out_specs=(image_spec, text_spec, P()),
        check_vma=False,
    )
```

```python
import functools
import math
import jax
import jax.numpy as jnp
from jax import lax
from jax.experimental import pallas as pl
from jax.experimental.pallas import tpu as pltpu
from jax.sharding import Mesh, PartitionSpec as P

EPS = 1e-06
EXTRA = 128
F32 = jnp.float32
BF16 = jnp.bfloat16
IMAGE_ORDER = ("zh", "z0", "xl", "core", "xh", "yh", "y0")
TEXT_ORDER = ("xh", "yh", "y0", "zh", "z0", "xl", "core")
TEXT_GROUP = ("xh", "xl", "yh")
IMAGE_GROUP = ("zh", "y0")
PAIR = "z0"
VMEM = pl.BlockSpec(memory_space=pltpu.VMEM)
SMEM = pl.BlockSpec(memory_space=pltpu.SMEM)


def unit_and_norm(rows):
    values = rows.astype(F32)
    norm = jnp.sqrt(jnp.sum(values * values, axis=1, keepdims=True) + EPS)
    return values / norm, norm


def lanes(rows):
    return lax.broadcasted_iota(jnp.int32, (rows, EXTRA), 1)


def pack_image_kernel(image_ref, pair_ref, image_out, image_unit, image_norm):
    rows, width = image_ref.shape
    image_unit[...], image_norm[...] = unit_and_norm(image_ref[...])
    row = lax.broadcasted_iota(jnp.int32, (rows, EXTRA), 0)
    pair = jnp.zeros((rows, EXTRA), jnp.int32)
    for r in range(rows):
        pair = jnp.where(row == r, pair_ref[r], pair)
    lane = lanes(rows)
    high = lax.shift_right_logical(pair, 7)
    low = lax.bitwise_and(pair, 127)
    extra = jnp.where(lane == 0, high, jnp.where(lane == 1, low, 0)).astype(F32)
    image_two = jnp.concatenate([image_unit[...]] * 2, axis=0).astype(BF16)
    extra_two = jnp.concatenate([extra] * 2, axis=0).astype(BF16)
    step = 2 * rows
    for k in range(image_out.shape[0] // step):
        image_out[k * step : (k + 1) * step, :width] = image_two
        image_out[k * step : (k + 1) * step, width:] = extra_two


def pack_text_kernel(text_ref, text_out, text_unit, text_norm):
    text_unit[...], text_norm[...] = unit_and_norm(text_ref[...])
    text_two = jnp.concatenate([text_unit[...]] * 2, axis=0).astype(BF16)
    step = text_two.shape[0]
    for k in range(text_out.shape[0] // step):
        text_out[k * step : (k + 1) * step, :] = text_two


def split_stats(lane, first, values):
    out = jnp.zeros(lane.shape, F32)
    for n, value in enumerate(values):
        high = value.astype(BF16).astype(F32)
        out = jnp.where(lane == first + n, high, out)
        out = jnp.where(lane == first + 3 + n, value - high, out)
    return out


def text_columns(own_rows, sizes, count):
    place = lax.broadcasted_iota(jnp.int32, (1, count), 1)
    peer, row = place // own_rows, place % own_rows
    index = {a: lax.axis_index(a) for a in IMAGE_GROUP + (PAIR, "core")}
    for a in reversed(TEXT_GROUP):
        index[a] = peer % sizes[a]
        peer = peer // sizes[a]
    owner = 0
    for a in TEXT_ORDER:
        owner = owner * sizes[a] + index[a]
    return owner * own_rows + row


def stacked(piece_refs, cols):
    return jnp.concatenate([r[:, cols] for r in piece_refs], axis=0)


def scale_of(log_scale_ref):
    return jnp.exp(jnp.zeros((8, 128), F32) + log_scale_ref[0])[0:1, 0:1]


def score_kernel(own_rows, sizes, piece_refs, text_ref, log_scale_ref, bias_ref, text_out, low_out, along_out):
    text = text_ref[...]
    count, width = text.shape
    scale = scale_of(log_scale_ref)
    column = text_columns(own_rows, sizes, count).astype(F32)
    image = stacked(piece_refs, slice(0, width))
    extra = stacked(piece_refs, slice(width, width + EXTRA)).astype(F32)
    pair = extra[:, 0:1] * 128.0 + extra[:, 1:2]
    cosine = lax.dot_general(image, text, (((1,), (1,)), ((), ())), preferred_element_type=F32)
    scaled = scale * cosine
    logits = scaled + bias_ref[0]
    match = pair == column
    arg = jnp.where(match, -logits, logits)
    small = jnp.exp(-jnp.abs(arg))
    inverse = 1.0 / (1.0 + small)
    prob = jnp.where(arg >= 0, inverse, small * inverse)
    dlogit = jnp.where(match, -prob, prob)
    loss = jnp.maximum(arg, 0.0) + jnp.log1p(small)
    low = dlogit.astype(BF16)
    product = low.astype(F32) * scaled
    totals = [jnp.sum(v, axis=(0, 1), keepdims=True) for v in (loss, dlogit, dlogit * scaled)]
    low_out[...] = low
    along_image = jnp.sum(product, axis=1, keepdims=True)
    along_out[...] = jnp.where(lanes(image.shape[0]) == 0, along_image, 0.0)
    along_text = jnp.broadcast_to(jnp.sum(product, axis=0, keepdims=True), (128, count)).T
    along_text = along_text.astype(BF16).astype(F32)
    low_turned = dlogit.T.astype(BF16)
    block = width // 3
    for first in range(0, width, block):
        cols = slice(first, first + block)
        part = scale * jnp.dot(low_turned, image[:, cols], preferred_element_type=F32)
        text_out[:, cols] = (part - along_text[:, 0:1] * text[:, cols].astype(F32)).astype(BF16)
    lane = lanes(count)
    stats = split_stats(lane, 1, [jnp.broadcast_to(t, lane.shape) for t in totals])
    text_out[:, width:] = jnp.where(lane == 0, along_text, stats).astype(BF16)


def image_kernel(piece_refs, text_ref, low_ref, along_ref, log_scale_ref, stay_out, away_out):
    width = text_ref.shape[1]
    scale = scale_of(log_scale_ref)
    half = low_ref.shape[0] // 2
    for target, pieces, rows in (
        (away_out, piece_refs[2:], slice(half, 2 * half)),
        (stay_out, piece_refs[:2], slice(0, half)),
    ):
        low, along = low_ref[rows, :], along_ref[rows, :]
        block = width // 3
        for first in range(0, width, block):
            cols = slice(first, first + block)
            part = scale * jnp.dot(low, text_ref[:, cols], preferred_element_type=F32)
            target[:, cols] = part - along[:, 0:1] * stacked(pieces, cols).astype(F32)
        target[:, width:] = along


def merge_stats(extra, rows):
    peers = extra.shape[0] // rows
    total = jnp.sum(extra.reshape(peers, rows, EXTRA), axis=0)
    return [total[0:1, n : n + 1] + total[0:1, n + 3 : n + 4] for n in (1, 2, 3)]


def add_kernel(stay_ref, came_ref, keep_out, send_out):
    half = keep_out.shape[0]
    keep_out[...] = stay_ref[:half, :] + came_ref[:half, :]
    send_out[...] = (stay_ref[half:, :] + came_ref[half:, :]).astype(BF16)


def join_kernel(own_rows, keep_ref, came_ref, text_back_ref, out_ref):
    width = keep_ref.shape[1] - EXTRA
    out_ref[:, :width] = (keep_ref[:, :width] + came_ref[:, :width].astype(F32)).astype(BF16)
    lane = lanes(keep_ref.shape[0])
    stats = merge_stats(text_back_ref[:, width:].astype(F32), own_rows)
    stats = split_stats(lane, 1, [jnp.broadcast_to(t, lane.shape) for t in stats])
    along = keep_ref[:, width:] + came_ref[:, width:].astype(F32)
    out_ref[:, width:] = jnp.where(lane == 0, along, stats).astype(BF16)


def finish_kernel(parts_ref, unit_ref, norm_ref, grad_out):
    rows, width = unit_ref.shape
    peers = parts_ref.shape[0] // rows
    total = jnp.sum(parts_ref[...].astype(F32).reshape(peers, rows, width + EXTRA), axis=0)
    unit = unit_ref[...]
    grad = total[:, :width] + total[:, width : width + 1] * unit.astype(BF16).astype(F32)
    grad_out[...] = (grad - unit * jnp.sum(unit * grad, axis=1, keepdims=True)) / norm_ref[...]


def stats_kernel(own_rows, batch, parts_ref, out_ref):
    width = parts_ref.shape[1] - EXTRA
    lane = lanes(8)
    out = jnp.zeros(lane.shape, F32)
    for n, value in enumerate(merge_stats(parts_ref[:, width:].astype(F32), own_rows)):
        out = jnp.where(lane == n, value / batch, out)
    out_ref[...] = jnp.broadcast_to(out[None], out_ref.shape)


def shape(*dims, dtype=BF16):
    return jax.ShapeDtypeStruct(dims, dtype)


def call(kernel, outs, *args, scalars=0, flops=0, limit=40 * 1024 * 1024):
    size = sum(a.size * a.dtype.itemsize for a in args)
    return pl.pallas_call(
        kernel,
        out_shape=outs,
        in_specs=[VMEM] * (len(args) - scalars) + [SMEM] * scalars,
        out_specs=jax.tree.map(lambda _: VMEM, outs),
        cost_estimate=pl.CostEstimate(flops=flops, bytes_accessed=4 * size, transcendentals=0),
        compiler_params=pltpu.CompilerParams(vmem_limit_bytes=limit),
    )(*args)


def per_device(image_embed, text_embed, pair_index, log_scale, bias):
    own_rows, width = image_embed.shape
    sizes = {a: lax.axis_size(a) for a in IMAGE_ORDER}
    wide = width + EXTRA
    row_count = math.prod(sizes[a] for a in IMAGE_GROUP) * own_rows
    text_count = math.prod(sizes[a] for a in TEXT_GROUP) * own_rows
    unit_shape, norm_shape = shape(own_rows, width, dtype=F32), shape(own_rows, 1, dtype=F32)
    image_send, image_unit, image_norm = call(
        pack_image_kernel, (shape(row_count, wide), unit_shape, norm_shape),
        image_embed, pair_index, scalars=1, limit=None,
    )
    text_send, text_unit, text_norm = call(
        pack_text_kernel, (shape(text_count, width), unit_shape, norm_shape), text_embed, limit=None
    )
    piece = lax.all_to_all(image_send, IMAGE_GROUP, 0, 0, tiled=True)
    text = lax.all_to_all(text_send, TEXT_GROUP, 0, 0, tiled=True)
    swap = [(0, 1), (1, 0)]
    piece_pair = lax.ppermute(piece, PAIR, swap)
    piece_core = lax.ppermute(piece, "core", swap)
    piece_both = lax.ppermute(piece_pair, "core", swap)

    def score(a, b, c, d, *rest):
        score_kernel(own_rows, sizes, (a, b, c, d), *rest)

    def image_partials(a, b, c, d, *rest):
        image_kernel((a, b, c, d), *rest)

    pieces = (piece, piece_pair, piece_core, piece_both)
    work = 2 * 4 * row_count * text_count * width
    text_parts, low, along = call(
        score,
        (shape(text_count, wide), shape(4 * row_count, text_count), shape(4 * row_count, EXTRA, dtype=F32)),
        *pieces, text, log_scale, bias, scalars=2, flops=2 * work,
    )
    text_back = lax.all_to_all(text_parts, TEXT_GROUP, 0, 0, tiled=True)
    half = shape(2 * row_count, wide, dtype=F32)
    stay, away = call(image_partials, (half, half), *pieces, text, low, along, log_scale, scalars=1, flops=work)
    came = lax.ppermute(away, "core", swap)
    keep, send = call(
        add_kernel, (shape(row_count, wide, dtype=F32), shape(row_count, wide)), stay, came
    )
    came_pair = lax.ppermute(send, PAIR, swap)
    image_parts = call(
        functools.partial(join_kernel, own_rows), shape(row_count, wide), keep, came_pair, text_back
    )
    image_back = lax.all_to_all(image_parts, IMAGE_GROUP, 0, 0, tiled=True)
    text_grad = call(finish_kernel, unit_shape, text_back, text_unit, text_norm)
    four = sizes[PAIR] * sizes["core"]
    batch = own_rows * math.prod(sizes.values())
    sums = call(functools.partial(stats_kernel, own_rows, batch), shape(four, 8, EXTRA, dtype=F32), image_back)
    sums = lax.all_to_all(sums, (PAIR, "core"), 0, 0, tiled=True)
    image_grad = call(finish_kernel, unit_shape, image_back, image_unit, image_norm)
    stats = jnp.sum(sums[:, 0, :3], axis=0)
    return (image_grad, text_grad, stats)


def solution(mesh):
    img, txt = mesh.shape["img"], mesh.shape["txt"]
    parts = (img // 16, 2, 4, 2, 2, txt // 4, 2)
    split = Mesh(mesh.devices.reshape(parts), IMAGE_ORDER)
    image_spec, text_spec = P(IMAGE_ORDER, None), P(TEXT_ORDER, None)
    return jax.shard_map(
        per_device,
        mesh=split,
        in_specs=(image_spec, text_spec, P(IMAGE_ORDER), P(), P()),
        out_specs=(image_spec, text_spec, P()),
        check_vma=False,
    )
```

```python
import functools
import math
import jax
import jax.numpy as jnp
from jax import lax
from jax.experimental import pallas as pl
from jax.experimental.pallas import tpu as pltpu
from jax.sharding import Mesh, PartitionSpec as P

EPS = 1e-06
EXTRA = 128
F32 = jnp.float32
BF16 = jnp.bfloat16
IMAGE_ORDER = ("zh", "z0", "x1", "x0", "core", "xh", "yh", "y0")
TEXT_ORDER = ("xh", "yh", "y0", "zh", "z0", "x1", "x0", "core")
TEXT_GROUP = ("xh", "x1", "x0", "z0")
IMAGE_GROUP = ("zh", "yh")
PAIR = "y0"
VMEM = pl.BlockSpec(memory_space=pltpu.VMEM)
SMEM = pl.BlockSpec(memory_space=pltpu.SMEM)


def unit_and_norm(rows):
    values = rows.astype(F32)
    norm = jnp.sqrt(jnp.sum(values * values, axis=1, keepdims=True) + EPS)
    return values / norm, norm


def lanes(rows):
    return lax.broadcasted_iota(jnp.int32, (rows, EXTRA), 1)


def pack_image_kernel(image_ref, pair_ref, image_out, image_unit, image_norm):
    rows, width = image_ref.shape
    image_unit[...], image_norm[...] = unit_and_norm(image_ref[...])
    row = lax.broadcasted_iota(jnp.int32, (rows, EXTRA), 0)
    pair = jnp.zeros((rows, EXTRA), jnp.int32)
    for r in range(rows):
        pair = jnp.where(row == r, pair_ref[r], pair)
    lane = lanes(rows)
    high = lax.shift_right_logical(pair, 7)
    low = lax.bitwise_and(pair, 127)
    extra = jnp.where(lane == 0, high, jnp.where(lane == 1, low, 0)).astype(F32)
    image_two = jnp.concatenate([image_unit[...]] * 2, axis=0).astype(BF16)
    extra_two = jnp.concatenate([extra] * 2, axis=0).astype(BF16)
    step = 2 * rows
    for k in range(image_out.shape[0] // step):
        image_out[k * step : (k + 1) * step, :width] = image_two
        image_out[k * step : (k + 1) * step, width:] = extra_two


def pack_text_kernel(text_ref, text_out, text_unit, text_norm):
    text_unit[...], text_norm[...] = unit_and_norm(text_ref[...])
    text_two = jnp.concatenate([text_unit[...]] * 2, axis=0).astype(BF16)
    step = text_two.shape[0]
    for k in range(text_out.shape[0] // step):
        text_out[k * step : (k + 1) * step, :] = text_two


def split_stats(lane, first, values):
    out = jnp.zeros(lane.shape, F32)
    for n, value in enumerate(values):
        high = value.astype(BF16).astype(F32)
        out = jnp.where(lane == first + n, high, out)
        out = jnp.where(lane == first + 3 + n, value - high, out)
    return out


def text_columns(own_rows, sizes, count):
    place = lax.broadcasted_iota(jnp.int32, (1, 2 * count), 1)
    away = place // count
    peer, row = (place % count) // own_rows, place % own_rows
    index = {a: lax.axis_index(a) for a in IMAGE_GROUP + (PAIR, "core")}
    index["core"] = index["core"] + away - 2 * index["core"] * away
    for a in reversed(TEXT_GROUP):
        index[a] = peer % sizes[a]
        peer = peer // sizes[a]
    owner = 0
    for a in TEXT_ORDER:
        owner = owner * sizes[a] + index[a]
    return owner * own_rows + row


def stacked(piece_refs, cols):
    return jnp.concatenate([r[:, cols] for r in piece_refs], axis=0)


def scale_of(log_scale_ref):
    return jnp.exp(jnp.zeros((8, 128), F32) + log_scale_ref[0])[0:1, 0:1]


def score_kernel(
    own_rows, sizes, image_refs, text_refs, log_scale_ref, bias_ref, away_out, stay_out, low_out, along_out
):
    count, width = text_refs[0].shape
    scale = scale_of(log_scale_ref)
    column = text_columns(own_rows, sizes, count).astype(F32)
    image = stacked(image_refs, slice(0, width))
    text = stacked(text_refs, slice(0, width))
    extra = stacked(image_refs, slice(width, width + EXTRA)).astype(F32)
    pair = extra[:, 0:1] * 128.0 + extra[:, 1:2]
    cosine = lax.dot_general(image, text, (((1,), (1,)), ((), ())), preferred_element_type=F32)
    scaled = scale * cosine
    logits = scaled + bias_ref[0]
    match = pair == column
    arg = jnp.where(match, -logits, logits)
    small = jnp.exp(-jnp.abs(arg))
    inverse = 1.0 / (1.0 + small)
    prob = jnp.where(arg >= 0, inverse, small * inverse)
    dlogit = jnp.where(match, -prob, prob)
    loss = jnp.maximum(arg, 0.0) + jnp.log1p(small)
    low = dlogit.astype(BF16)
    product = low.astype(F32) * scaled
    totals = [jnp.sum(v, axis=(0, 1), keepdims=True) for v in (loss, dlogit, dlogit * scaled)]
    low_out[...] = low
    along_image = jnp.sum(product, axis=1, keepdims=True)
    along_out[...] = jnp.where(lanes(image.shape[0]) == 0, along_image, 0.0)
    along_text = jnp.broadcast_to(jnp.sum(product, axis=0, keepdims=True), (128, 2 * count)).T
    low_turned = dlogit.T.astype(BF16)
    lane = lanes(count)
    block = width // 3
    for target, rows in ((away_out, slice(count, 2 * count)), (stay_out, slice(0, count))):
        along = along_text[rows, 0:1]
        for first in range(0, width, block):
            cols = slice(first, first + block)
            part = scale * jnp.dot(low_turned[rows], image[:, cols], preferred_element_type=F32)
            target[:, cols] = part - along * text[rows, cols].astype(F32)
        kept = jnp.where(lane == 0, along, 0.0)
        for n, total in enumerate(totals):
            kept = jnp.where(lane == 1 + n, total, kept)
        target[:, width:] = kept


def join_text_kernel(stay_ref, came_ref, out_ref):
    width = stay_ref.shape[1] - EXTRA
    out_ref[:, :width] = (stay_ref[:, :width] + came_ref[:, :width]).astype(BF16)
    lane = lanes(stay_ref.shape[0])
    extra = stay_ref[:, width:] + came_ref[:, width:]
    stats = split_stats(lane, 1, [jnp.broadcast_to(extra[:, n : n + 1], lane.shape) for n in (1, 2, 3)])
    out_ref[:, width:] = jnp.where(lane == 0, extra, stats).astype(BF16)


def image_kernel(image_refs, text_refs, low_ref, along_ref, log_scale_ref, away_out, stay_out):
    count, width = text_refs[0].shape
    scale = scale_of(log_scale_ref)
    half = low_ref.shape[0] // 2
    for target, image_ref, rows in (
        (away_out, image_refs[1], slice(half, 2 * half)),
        (stay_out, image_refs[0], slice(0, half)),
    ):
        low, along = low_ref[rows, :], along_ref[rows, :]
        block = width // 3
        for first in range(0, width, block):
            cols = slice(first, first + block)
            part = scale * jnp.dot(low, stacked(text_refs, cols), preferred_element_type=F32)
            part = part - along[:, 0:1] * image_ref[:, cols].astype(F32)
            target[:, cols] = part.astype(target.dtype)
        target[:, width:] = along.astype(target.dtype)


def merge_stats(extra, rows):
    peers = extra.shape[0] // rows
    total = jnp.sum(extra.reshape(peers, rows, EXTRA), axis=0)
    return [total[0:1, n : n + 1] + total[0:1, n + 3 : n + 4] for n in (1, 2, 3)]


def join_kernel(own_rows, keep_ref, came_ref, text_back_ref, out_ref):
    width = keep_ref.shape[1] - EXTRA
    out_ref[:, :width] = (keep_ref[:, :width] + came_ref[:, :width].astype(F32)).astype(BF16)
    lane = lanes(keep_ref.shape[0])
    stats = merge_stats(text_back_ref[:, width:].astype(F32), own_rows)
    stats = split_stats(lane, 1, [jnp.broadcast_to(t, lane.shape) for t in stats])
    along = keep_ref[:, width:] + came_ref[:, width:].astype(F32)
    out_ref[:, width:] = jnp.where(lane == 0, along, stats).astype(BF16)


def finish_kernel(parts_ref, unit_ref, norm_ref, grad_out):
    rows, width = unit_ref.shape
    peers = parts_ref.shape[0] // rows
    total = jnp.sum(parts_ref[...].astype(F32).reshape(peers, rows, width + EXTRA), axis=0)
    unit = unit_ref[...]
    grad = total[:, :width] + total[:, width : width + 1] * unit.astype(BF16).astype(F32)
    grad_out[...] = (grad - unit * jnp.sum(unit * grad, axis=1, keepdims=True)) / norm_ref[...]


def stats_kernel(own_rows, batch, parts_ref, out_ref):
    width = parts_ref.shape[1] - EXTRA
    lane = lanes(8)
    out = jnp.zeros(lane.shape, F32)
    for n, value in enumerate(merge_stats(parts_ref[:, width:].astype(F32), own_rows)):
        out = jnp.where(lane == n, value / batch, out)
    out_ref[...] = out


def shape(*dims, dtype=BF16):
    return jax.ShapeDtypeStruct(dims, dtype)


def call(kernel, outs, *args, scalars=0, flops=0, limit=40 * 1024 * 1024):
    size = sum(a.size * a.dtype.itemsize for a in args)
    return pl.pallas_call(
        kernel,
        out_shape=outs,
        in_specs=[VMEM] * (len(args) - scalars) + [SMEM] * scalars,
        out_specs=jax.tree.map(lambda _: VMEM, outs),
        cost_estimate=pl.CostEstimate(flops=flops, bytes_accessed=4 * size, transcendentals=0),
        compiler_params=pltpu.CompilerParams(vmem_limit_bytes=limit),
    )(*args)


def per_device(image_embed, text_embed, pair_index, log_scale, bias):
    own_rows, width = image_embed.shape
    sizes = {a: lax.axis_size(a) for a in IMAGE_ORDER}
    wide = width + EXTRA
    row_count = math.prod(sizes[a] for a in IMAGE_GROUP) * own_rows
    text_count = math.prod(sizes[a] for a in TEXT_GROUP) * own_rows
    unit_shape, norm_shape = shape(own_rows, width, dtype=F32), shape(own_rows, 1, dtype=F32)
    image_send, image_unit, image_norm = call(
        pack_image_kernel, (shape(row_count, wide), unit_shape, norm_shape),
        image_embed, pair_index, scalars=1, limit=None,
    )
    text_send, text_unit, text_norm = call(
        pack_text_kernel, (shape(text_count, width), unit_shape, norm_shape), text_embed, limit=None
    )
    swap = [(0, 1), (1, 0)]
    piece = lax.all_to_all(image_send, IMAGE_GROUP, 0, 0, tiled=True)
    text = lax.all_to_all(text_send, TEXT_GROUP, 0, 0, tiled=True)
    piece_pair = lax.ppermute(piece, PAIR, swap)
    text_core = lax.ppermute(text, "core", swap)
    held = (piece, piece_pair, text, text_core)

    def score(a, b, c, d, *rest):
        score_kernel(own_rows, sizes, (a, b), (c, d), *rest)

    def image_partials(a, b, c, d, *rest):
        image_kernel((a, b), (c, d), *rest)

    work = 2 * 4 * row_count * text_count * width
    text_half = shape(text_count, wide, dtype=F32)
    away, stay, low, along = call(
        score,
        (text_half, text_half, shape(2 * row_count, 2 * text_count), shape(2 * row_count, EXTRA, dtype=F32)),
        *held, log_scale, bias, scalars=2, flops=2 * work,
    )
    came = lax.ppermute(away, "core", swap)
    send, keep = call(
        image_partials,
        (shape(row_count, wide), shape(row_count, wide, dtype=F32)),
        *held, low, along, log_scale, scalars=1, flops=work,
    )
    text_parts = call(join_text_kernel, shape(text_count, wide), stay, came)
    text_back = lax.all_to_all(text_parts, TEXT_GROUP, 0, 0, tiled=True)
    came_pair = lax.ppermute(send, PAIR, swap)
    image_parts = call(
        functools.partial(join_kernel, own_rows), shape(row_count, wide), keep, came_pair, text_back
    )
    image_back = lax.all_to_all(image_parts, IMAGE_GROUP, 0, 0, tiled=True)
    text_grad = call(finish_kernel, unit_shape, text_back, text_unit, text_norm)
    batch = own_rows * math.prod(sizes.values())
    sums = call(functools.partial(stats_kernel, own_rows, batch), shape(8, EXTRA, dtype=F32), image_back)
    sums_came = lax.ppermute(sums, PAIR, swap)
    image_grad = call(finish_kernel, unit_shape, image_back, image_unit, image_norm)
    stats = (sums + sums_came)[0, :3]
    return (image_grad, text_grad, stats)


def solution(mesh):
    img, txt = mesh.shape["img"], mesh.shape["txt"]
    parts = (img // 16, 2, 2, 2, 2, 2, txt // 4, 2)
    split = Mesh(mesh.devices.reshape(parts), IMAGE_ORDER)
    image_spec, text_spec = P(IMAGE_ORDER, None), P(TEXT_ORDER, None)
    return jax.shard_map(
        per_device,
        mesh=split,
        in_specs=(image_spec, text_spec, P(IMAGE_ORDER), P(), P()),
        out_specs=(image_spec, text_spec, P()),
        check_vma=False,
    )
```

```python
import functools
import math
import jax
import jax.numpy as jnp
from jax import lax
from jax.experimental import pallas as pl
from jax.experimental.pallas import tpu as pltpu
from jax.sharding import Mesh, PartitionSpec as P

EPS = 1e-06
EXTRA = 128
F32 = jnp.float32
BF16 = jnp.bfloat16
IMAGE_ORDER = ("zh", "z0", "x1", "x0", "core", "xh", "yh", "y0")
TEXT_ORDER = ("xh", "yh", "y0", "zh", "z0", "x1", "x0", "core")
TEXT_GROUP = ("xh", "x1", "zh")
IMAGE_GROUP = ("x0", "z0", "yh")
PAIR = "y0"
VMEM = pl.BlockSpec(memory_space=pltpu.VMEM)
SMEM = pl.BlockSpec(memory_space=pltpu.SMEM)


def unit_and_norm(rows):
    values = rows.astype(F32)
    norm = jnp.sqrt(jnp.sum(values * values, axis=1, keepdims=True) + EPS)
    return values / norm, norm


def lanes(rows):
    return lax.broadcasted_iota(jnp.int32, (rows, EXTRA), 1)


def pack_image_kernel(image_ref, pair_ref, image_out, image_unit, image_norm):
    rows, width = image_ref.shape
    image_unit[...], image_norm[...] = unit_and_norm(image_ref[...])
    row = lax.broadcasted_iota(jnp.int32, (rows, EXTRA), 0)
    pair = jnp.zeros((rows, EXTRA), jnp.int32)
    for r in range(rows):
        pair = jnp.where(row == r, pair_ref[r], pair)
    lane = lanes(rows)
    high = lax.shift_right_logical(pair, 7)
    low = lax.bitwise_and(pair, 127)
    extra = jnp.where(lane == 0, high, jnp.where(lane == 1, low, 0)).astype(F32)
    image_two = jnp.concatenate([image_unit[...]] * 2, axis=0).astype(BF16)
    extra_two = jnp.concatenate([extra] * 2, axis=0).astype(BF16)
    step = 2 * rows
    for k in range(image_out.shape[0] // step):
        image_out[k * step : (k + 1) * step, :width] = image_two
        image_out[k * step : (k + 1) * step, width:] = extra_two


def pack_text_kernel(text_ref, text_out, text_unit, text_norm):
    text_unit[...], text_norm[...] = unit_and_norm(text_ref[...])
    text_two = jnp.concatenate([text_unit[...]] * 2, axis=0).astype(BF16)
    step = text_two.shape[0]
    for k in range(text_out.shape[0] // step):
        text_out[k * step : (k + 1) * step, :] = text_two


def split_stats(lane, first, values):
    out = jnp.zeros(lane.shape, F32)
    for n, value in enumerate(values):
        high = value.astype(BF16).astype(F32)
        out = jnp.where(lane == first + n, high, out)
        out = jnp.where(lane == first + 3 + n, value - high, out)
    return out


def text_columns(own_rows, sizes, count):
    place = lax.broadcasted_iota(jnp.int32, (1, 2 * count), 1)
    away = place // count
    peer, row = (place % count) // own_rows, place % own_rows
    index = {a: lax.axis_index(a) for a in IMAGE_GROUP + (PAIR, "core")}
    index["core"] = index["core"] + away - 2 * index["core"] * away
    for a in reversed(TEXT_GROUP):
        index[a] = peer % sizes[a]
        peer = peer // sizes[a]
    owner = 0
    for a in TEXT_ORDER:
        owner = owner * sizes[a] + index[a]
    return owner * own_rows + row


def stacked(piece_refs, cols):
    return jnp.concatenate([r[:, cols] for r in piece_refs], axis=0)


def scale_of(log_scale_ref):
    return jnp.exp(jnp.zeros((8, 128), F32) + log_scale_ref[0])[0:1, 0:1]


def score_kernel(
    own_rows, sizes, image_refs, text_refs, log_scale_ref, bias_ref, away_out, stay_out, low_out, along_out
):
    count, width = text_refs[0].shape
    scale = scale_of(log_scale_ref)
    column = text_columns(own_rows, sizes, count).astype(F32)
    image = stacked(image_refs, slice(0, width))
    text = stacked(text_refs, slice(0, width))
    extra = stacked(image_refs, slice(width, width + EXTRA)).astype(F32)
    pair = extra[:, 0:1] * 128.0 + extra[:, 1:2]
    cosine = lax.dot_general(image, text, (((1,), (1,)), ((), ())), preferred_element_type=F32)
    scaled = scale * cosine
    logits = scaled + bias_ref[0]
    match = pair == column
    arg = jnp.where(match, -logits, logits)
    small = jnp.exp(-jnp.abs(arg))
    inverse = 1.0 / (1.0 + small)
    prob = jnp.where(arg >= 0, inverse, small * inverse)
    dlogit = jnp.where(match, -prob, prob)
    loss = jnp.maximum(arg, 0.0) + jnp.log1p(small)
    low = dlogit.astype(BF16)
    product = low.astype(F32) * scaled
    totals = [jnp.sum(v, axis=(0, 1), keepdims=True) for v in (loss, dlogit, dlogit * scaled)]
    low_out[...] = low
    along_image = jnp.sum(product, axis=1, keepdims=True)
    along_out[...] = jnp.where(lanes(image.shape[0]) == 0, along_image, 0.0)
    along_text = jnp.broadcast_to(jnp.sum(product, axis=0, keepdims=True), (128, 2 * count)).T
    low_turned = dlogit.T.astype(BF16)
    lane = lanes(count)
    block = width // 3
    for target, rows in ((away_out, slice(count, 2 * count)), (stay_out, slice(0, count))):
        along = along_text[rows, 0:1]
        for first in range(0, width, block):
            cols = slice(first, first + block)
            part = scale * jnp.dot(low_turned[rows], image[:, cols], preferred_element_type=F32)
            target[:, cols] = part - along * text[rows, cols].astype(F32)
        kept = jnp.where(lane == 0, along, 0.0)
        for n, total in enumerate(totals):
            kept = jnp.where(lane == 1 + n, total, kept)
        target[:, width:] = kept


def join_text_kernel(stay_ref, came_ref, out_ref):
    width = stay_ref.shape[1] - EXTRA
    out_ref[:, :width] = (stay_ref[:, :width] + came_ref[:, :width]).astype(BF16)
    lane = lanes(stay_ref.shape[0])
    extra = stay_ref[:, width:] + came_ref[:, width:]
    stats = split_stats(lane, 1, [jnp.broadcast_to(extra[:, n : n + 1], lane.shape) for n in (1, 2, 3)])
    out_ref[:, width:] = jnp.where(lane == 0, extra, stats).astype(BF16)


def image_kernel(image_refs, text_refs, low_ref, along_ref, log_scale_ref, away_out, stay_out):
    count, width = text_refs[0].shape
    scale = scale_of(log_scale_ref)
    half = low_ref.shape[0] // 2
    for target, image_ref, rows in (
        (away_out, image_refs[1], slice(half, 2 * half)),
        (stay_out, image_refs[0], slice(0, half)),
    ):
        low, along = low_ref[rows, :], along_ref[rows, :]
        block = width // 3
        for first in range(0, width, block):
            cols = slice(first, first + block)
            part = scale * jnp.dot(low, stacked(text_refs, cols), preferred_element_type=F32)
            part = part - along[:, 0:1] * image_ref[:, cols].astype(F32)
            target[:, cols] = part.astype(target.dtype)
        target[:, width:] = along.astype(target.dtype)


def merge_stats(extra, rows):
    peers = extra.shape[0] // rows
    total = jnp.sum(extra.reshape(peers, rows, EXTRA), axis=0)
    return [total[0:1, n : n + 1] + total[0:1, n + 3 : n + 4] for n in (1, 2, 3)]


def join_kernel(own_rows, keep_ref, came_ref, text_back_ref, out_ref):
    width = keep_ref.shape[1] - EXTRA
    out_ref[:, :width] = (keep_ref[:, :width] + came_ref[:, :width].astype(F32)).astype(BF16)
    lane = lanes(keep_ref.shape[0])
    stats = merge_stats(text_back_ref[:, width:].astype(F32), own_rows)
    stats = split_stats(lane, 1, [jnp.broadcast_to(t, lane.shape) for t in stats])
    along = keep_ref[:, width:] + came_ref[:, width:].astype(F32)
    out_ref[:, width:] = jnp.where(lane == 0, along, stats).astype(BF16)


def finish_kernel(parts_ref, unit_ref, norm_ref, grad_out):
    rows, width = unit_ref.shape
    peers = parts_ref.shape[0] // rows
    total = jnp.sum(parts_ref[...].astype(F32).reshape(peers, rows, width + EXTRA), axis=0)
    unit = unit_ref[...]
    grad = total[:, :width] + total[:, width : width + 1] * unit.astype(BF16).astype(F32)
    grad_out[...] = (grad - unit * jnp.sum(unit * grad, axis=1, keepdims=True)) / norm_ref[...]


def stats_kernel(own_rows, batch, parts_ref, out_ref):
    width = parts_ref.shape[1] - EXTRA
    lane = lanes(8)
    out = jnp.zeros(lane.shape, F32)
    for n, value in enumerate(merge_stats(parts_ref[:, width:].astype(F32), own_rows)):
        out = jnp.where(lane == n, value / batch, out)
    out_ref[...] = out


def shape(*dims, dtype=BF16):
    return jax.ShapeDtypeStruct(dims, dtype)


def call(kernel, outs, *args, scalars=0, flops=0, limit=40 * 1024 * 1024):
    size = sum(a.size * a.dtype.itemsize for a in args)
    return pl.pallas_call(
        kernel,
        out_shape=outs,
        in_specs=[VMEM] * (len(args) - scalars) + [SMEM] * scalars,
        out_specs=jax.tree.map(lambda _: VMEM, outs),
        cost_estimate=pl.CostEstimate(flops=flops, bytes_accessed=4 * size, transcendentals=0),
        compiler_params=pltpu.CompilerParams(vmem_limit_bytes=limit),
    )(*args)


def per_device(image_embed, text_embed, pair_index, log_scale, bias):
    own_rows, width = image_embed.shape
    sizes = {a: lax.axis_size(a) for a in IMAGE_ORDER}
    wide = width + EXTRA
    row_count = math.prod(sizes[a] for a in IMAGE_GROUP) * own_rows
    text_count = math.prod(sizes[a] for a in TEXT_GROUP) * own_rows
    unit_shape, norm_shape = shape(own_rows, width, dtype=F32), shape(own_rows, 1, dtype=F32)
    image_send, image_unit, image_norm = call(
        pack_image_kernel, (shape(row_count, wide), unit_shape, norm_shape),
        image_embed, pair_index, scalars=1, limit=None,
    )
    text_send, text_unit, text_norm = call(
        pack_text_kernel, (shape(text_count, width), unit_shape, norm_shape), text_embed, limit=None
    )
    swap = [(0, 1), (1, 0)]
    piece = lax.all_to_all(image_send, IMAGE_GROUP, 0, 0, tiled=True)
    text = lax.all_to_all(text_send, TEXT_GROUP, 0, 0, tiled=True)
    piece_pair = lax.ppermute(piece, PAIR, swap)
    text_core = lax.ppermute(text, "core", swap)
    held = (piece, piece_pair, text, text_core)

    def score(a, b, c, d, *rest):
        score_kernel(own_rows, sizes, (a, b), (c, d), *rest)

    def image_partials(a, b, c, d, *rest):
        image_kernel((a, b), (c, d), *rest)

    work = 2 * 4 * row_count * text_count * width
    text_half = shape(text_count, wide, dtype=F32)
    away, stay, low, along = call(
        score,
        (text_half, text_half, shape(2 * row_count, 2 * text_count), shape(2 * row_count, EXTRA, dtype=F32)),
        *held, log_scale, bias, scalars=2, flops=2 * work,
    )
    came = lax.ppermute(away, "core", swap)
    send, keep = call(
        image_partials,
        (shape(row_count, wide), shape(row_count, wide, dtype=F32)),
        *held, low, along, log_scale, scalars=1, flops=work,
    )
    text_parts = call(join_text_kernel, shape(text_count, wide), stay, came)
    text_back = lax.all_to_all(text_parts, TEXT_GROUP, 0, 0, tiled=True)
    came_pair = lax.ppermute(send, PAIR, swap)
    image_parts = call(
        functools.partial(join_kernel, own_rows), shape(row_count, wide), keep, came_pair, text_back
    )
    image_back = lax.all_to_all(image_parts, IMAGE_GROUP, 0, 0, tiled=True)
    text_grad = call(finish_kernel, unit_shape, text_back, text_unit, text_norm)
    batch = own_rows * math.prod(sizes.values())
    sums = call(functools.partial(stats_kernel, own_rows, batch), shape(8, EXTRA, dtype=F32), image_back)
    sums_came = lax.ppermute(sums, PAIR, swap)
    image_grad = call(finish_kernel, unit_shape, image_back, image_unit, image_norm)
    stats = (sums + sums_came)[0, :3]
    return (image_grad, text_grad, stats)


def solution(mesh):
    img, txt = mesh.shape["img"], mesh.shape["txt"]
    parts = (img // 16, 2, 2, 2, 2, 2, txt // 4, 2)
    split = Mesh(mesh.devices.reshape(parts), IMAGE_ORDER)
    image_spec, text_spec = P(IMAGE_ORDER, None), P(TEXT_ORDER, None)
    return jax.shard_map(
        per_device,
        mesh=split,
        in_specs=(image_spec, text_spec, P(IMAGE_ORDER), P(), P()),
        out_specs=(image_spec, text_spec, P()),
        check_vma=False,
    )
```

```python
import functools
import math
import jax
import jax.numpy as jnp
from jax import lax
from jax.experimental import pallas as pl
from jax.experimental.pallas import tpu as pltpu
from jax.sharding import Mesh, PartitionSpec as P

EPS = 1e-06
EXTRA = 128
F32 = jnp.float32
BF16 = jnp.bfloat16
IMAGE_ORDER = ("zh", "z0", "x1", "x0", "core", "xh", "yh", "y0")
TEXT_ORDER = ("xh", "yh", "y0", "zh", "z0", "x1", "x0", "core")
TEXT_GROUP = ("xh", "x1", "zh")
IMAGE_GROUP = ("z0", "x0", "yh")
GATHER_GROUP = ("x0", "yh")
GATHER_PAIR = "z0"
PAIR = "y0"
VMEM = pl.BlockSpec(memory_space=pltpu.VMEM)
SMEM = pl.BlockSpec(memory_space=pltpu.SMEM)


def unit_and_norm(rows):
    values = rows.astype(F32)
    norm = jnp.sqrt(jnp.sum(values * values, axis=1, keepdims=True) + EPS)
    return values / norm, norm


def lanes(rows):
    return lax.broadcasted_iota(jnp.int32, (rows, EXTRA), 1)


def pack_image_kernel(image_ref, pair_ref, image_out, image_unit, image_norm):
    rows, width = image_ref.shape
    image_unit[...], image_norm[...] = unit_and_norm(image_ref[...])
    row = lax.broadcasted_iota(jnp.int32, (rows, EXTRA), 0)
    pair = jnp.zeros((rows, EXTRA), jnp.int32)
    for r in range(rows):
        pair = jnp.where(row == r, pair_ref[r], pair)
    lane = lanes(rows)
    high = lax.shift_right_logical(pair, 7)
    low = lax.bitwise_and(pair, 127)
    extra = jnp.where(lane == 0, high, jnp.where(lane == 1, low, 0)).astype(F32)
    image_two = jnp.concatenate([image_unit[...]] * 2, axis=0).astype(BF16)
    extra_two = jnp.concatenate([extra] * 2, axis=0).astype(BF16)
    step = 2 * rows
    for k in range(image_out.shape[0] // step):
        image_out[k * step : (k + 1) * step, :width] = image_two
        image_out[k * step : (k + 1) * step, width:] = extra_two


def pack_text_kernel(text_ref, text_out, text_unit, text_norm):
    text_unit[...], text_norm[...] = unit_and_norm(text_ref[...])
    text_two = jnp.concatenate([text_unit[...]] * 2, axis=0).astype(BF16)
    step = text_two.shape[0]
    for k in range(text_out.shape[0] // step):
        text_out[k * step : (k + 1) * step, :] = text_two


def split_stats(lane, first, values):
    out = jnp.zeros(lane.shape, F32)
    for n, value in enumerate(values):
        high = value.astype(BF16).astype(F32)
        out = jnp.where(lane == first + n, high, out)
        out = jnp.where(lane == first + 3 + n, value - high, out)
    return out


def text_columns(own_rows, sizes, count):
    place = lax.broadcasted_iota(jnp.int32, (1, 2 * count), 1)
    away = place // count
    peer, row = (place % count) // own_rows, place % own_rows
    index = {a: lax.axis_index(a) for a in IMAGE_GROUP + (PAIR, "core")}
    index["core"] = index["core"] + away - 2 * index["core"] * away
    for a in reversed(TEXT_GROUP):
        index[a] = peer % sizes[a]
        peer = peer // sizes[a]
    owner = 0
    for a in TEXT_ORDER:
        owner = owner * sizes[a] + index[a]
    return owner * own_rows + row


def stacked(piece_refs, cols):
    return jnp.concatenate([r[:, cols] for r in piece_refs], axis=0)


def in_order(refs, cols):
    first = lax.axis_index(GATHER_PAIR) == 0
    rows = []
    for own, other in zip(refs[::2], refs[1::2]):
        own, other = own[:, cols], other[:, cols]
        rows += [jnp.where(first, own, other), jnp.where(first, other, own)]
    return jnp.concatenate(rows, axis=0)


def scale_of(log_scale_ref):
    return jnp.exp(jnp.zeros((8, 128), F32) + log_scale_ref[0])[0:1, 0:1]


def score_kernel(
    own_rows, sizes, image_refs, text_refs, log_scale_ref, bias_ref, away_out, stay_out, low_out, along_out
):
    count, width = text_refs[0].shape
    scale = scale_of(log_scale_ref)
    column = text_columns(own_rows, sizes, count).astype(F32)
    image = in_order(image_refs, slice(0, width))
    text = stacked(text_refs, slice(0, width))
    extra = in_order(image_refs, slice(width, width + EXTRA)).astype(F32)
    pair = extra[:, 0:1] * 128.0 + extra[:, 1:2]
    cosine = lax.dot_general(image, text, (((1,), (1,)), ((), ())), preferred_element_type=F32)
    scaled = scale * cosine
    logits = scaled + bias_ref[0]
    match = pair == column
    arg = jnp.where(match, -logits, logits)
    small = jnp.exp(-jnp.abs(arg))
    inverse = 1.0 / (1.0 + small)
    prob = jnp.where(arg >= 0, inverse, small * inverse)
    dlogit = jnp.where(match, -prob, prob)
    loss = jnp.maximum(arg, 0.0) + jnp.log1p(small)
    low = dlogit.astype(BF16)
    product = low.astype(F32) * scaled
    totals = [jnp.sum(v, axis=(0, 1), keepdims=True) for v in (loss, dlogit, dlogit * scaled)]
    low_out[...] = low
    along_image = jnp.sum(product, axis=1, keepdims=True)
    along_out[...] = jnp.where(lanes(image.shape[0]) == 0, along_image, 0.0)
    along_text = jnp.broadcast_to(jnp.sum(product, axis=0, keepdims=True), (128, 2 * count)).T
    low_turned = dlogit.T.astype(BF16)
    lane = lanes(count)
    block = width // 3
    for target, rows in ((away_out, slice(count, 2 * count)), (stay_out, slice(0, count))):
        along = along_text[rows, 0:1]
        for first in range(0, width, block):
            cols = slice(first, first + block)
            part = scale * jnp.dot(low_turned[rows], image[:, cols], preferred_element_type=F32)
            target[:, cols] = part - along * text[rows, cols].astype(F32)
        kept = jnp.where(lane == 0, along, 0.0)
        for n, total in enumerate(totals):
            kept = jnp.where(lane == 1 + n, total, kept)
        target[:, width:] = kept


def join_text_kernel(stay_ref, came_ref, out_ref):
    width = stay_ref.shape[1] - EXTRA
    out_ref[:, :width] = (stay_ref[:, :width] + came_ref[:, :width]).astype(BF16)
    lane = lanes(stay_ref.shape[0])
    extra = stay_ref[:, width:] + came_ref[:, width:]
    stats = split_stats(lane, 1, [jnp.broadcast_to(extra[:, n : n + 1], lane.shape) for n in (1, 2, 3)])
    out_ref[:, width:] = jnp.where(lane == 0, extra, stats).astype(BF16)


def image_kernel(image_refs, text_refs, low_ref, along_ref, log_scale_ref, away_out, stay_out):
    count, width = text_refs[0].shape
    scale = scale_of(log_scale_ref)
    half = low_ref.shape[0] // 2
    for target, pieces, rows in (
        (away_out, image_refs[2:], slice(half, 2 * half)),
        (stay_out, image_refs[:2], slice(0, half)),
    ):
        low, along = low_ref[rows, :], along_ref[rows, :]
        block = width // 3
        for first in range(0, width, block):
            cols = slice(first, first + block)
            part = scale * jnp.dot(low, stacked(text_refs, cols), preferred_element_type=F32)
            part = part - along[:, 0:1] * in_order(pieces, cols).astype(F32)
            target[:, cols] = part.astype(target.dtype)
        target[:, width:] = along.astype(target.dtype)


def merge_stats(extra, rows):
    peers = extra.shape[0] // rows
    total = jnp.sum(extra.reshape(peers, rows, EXTRA), axis=0)
    return [total[0:1, n : n + 1] + total[0:1, n + 3 : n + 4] for n in (1, 2, 3)]


def join_kernel(own_rows, keep_ref, came_ref, text_back_ref, out_ref):
    width = keep_ref.shape[1] - EXTRA
    out_ref[:, :width] = (keep_ref[:, :width] + came_ref[:, :width].astype(F32)).astype(BF16)
    lane = lanes(keep_ref.shape[0])
    stats = merge_stats(text_back_ref[:, width:].astype(F32), own_rows)
    stats = split_stats(lane, 1, [jnp.broadcast_to(t, lane.shape) for t in stats])
    along = keep_ref[:, width:] + came_ref[:, width:].astype(F32)
    out_ref[:, width:] = jnp.where(lane == 0, along, stats).astype(BF16)


def finish_kernel(parts_ref, unit_ref, norm_ref, grad_out):
    rows, width = unit_ref.shape
    peers = parts_ref.shape[0] // rows
    total = jnp.sum(parts_ref[...].astype(F32).reshape(peers, rows, width + EXTRA), axis=0)
    unit = unit_ref[...]
    grad = total[:, :width] + total[:, width : width + 1] * unit.astype(BF16).astype(F32)
    grad_out[...] = (grad - unit * jnp.sum(unit * grad, axis=1, keepdims=True)) / norm_ref[...]


def stats_kernel(own_rows, batch, parts_ref, out_ref):
    width = parts_ref.shape[1] - EXTRA
    lane = lanes(8)
    out = jnp.zeros(lane.shape, F32)
    for n, value in enumerate(merge_stats(parts_ref[:, width:].astype(F32), own_rows)):
        out = jnp.where(lane == n, value / batch, out)
    out_ref[...] = out


def shape(*dims, dtype=BF16):
    return jax.ShapeDtypeStruct(dims, dtype)


def call(kernel, outs, *args, scalars=0, flops=0, limit=40 * 1024 * 1024):
    size = sum(a.size * a.dtype.itemsize for a in args)
    return pl.pallas_call(
        kernel,
        out_shape=outs,
        in_specs=[VMEM] * (len(args) - scalars) + [SMEM] * scalars,
        out_specs=jax.tree.map(lambda _: VMEM, outs),
        cost_estimate=pl.CostEstimate(flops=flops, bytes_accessed=4 * size, transcendentals=0),
        compiler_params=pltpu.CompilerParams(vmem_limit_bytes=limit),
    )(*args)


def per_device(image_embed, text_embed, pair_index, log_scale, bias):
    own_rows, width = image_embed.shape
    sizes = {a: lax.axis_size(a) for a in IMAGE_ORDER}
    wide = width + EXTRA
    row_count = math.prod(sizes[a] for a in IMAGE_GROUP) * own_rows
    text_count = math.prod(sizes[a] for a in TEXT_GROUP) * own_rows
    unit_shape, norm_shape = shape(own_rows, width, dtype=F32), shape(own_rows, 1, dtype=F32)
    gather_count = math.prod(sizes[a] for a in GATHER_GROUP) * own_rows
    image_send, image_unit, image_norm = call(
        pack_image_kernel, (shape(gather_count, wide), unit_shape, norm_shape),
        image_embed, pair_index, scalars=1, limit=None,
    )
    text_send, text_unit, text_norm = call(
        pack_text_kernel, (shape(text_count, width), unit_shape, norm_shape), text_embed, limit=None
    )
    swap = [(0, 1), (1, 0)]
    piece = lax.all_to_all(image_send, GATHER_GROUP, 0, 0, tiled=True)
    text = lax.all_to_all(text_send, TEXT_GROUP, 0, 0, tiled=True)
    piece_near = lax.ppermute(piece, GATHER_PAIR, swap)
    piece_pair = lax.ppermute(piece, PAIR, swap)
    piece_both = lax.ppermute(piece_near, PAIR, swap)
    text, piece_pair, piece_both = lax.optimization_barrier((text, piece_pair, piece_both))
    text_core = lax.ppermute(text, "core", swap)
    held = (piece, piece_near, piece_pair, piece_both, text, text_core)

    def score(*refs):
        score_kernel(own_rows, sizes, refs[:4], refs[4:6], *refs[6:])

    def image_partials(*refs):
        image_kernel(refs[:4], refs[4:6], *refs[6:])

    work = 2 * 4 * row_count * text_count * width
    text_half = shape(text_count, wide, dtype=F32)
    away, stay, low, along = call(
        score,
        (text_half, text_half, shape(2 * row_count, 2 * text_count), shape(2 * row_count, EXTRA, dtype=F32)),
        *held, log_scale, bias, scalars=2, flops=2 * work,
    )
    came = lax.ppermute(away, "core", swap)
    send, keep = call(
        image_partials,
        (shape(row_count, wide), shape(row_count, wide, dtype=F32)),
        *held, low, along, log_scale, scalars=1, flops=work,
    )
    text_parts = call(join_text_kernel, shape(text_count, wide), stay, came)
    text_back = lax.all_to_all(text_parts, TEXT_GROUP, 0, 0, tiled=True)
    came_pair = lax.ppermute(send, PAIR, swap)
    image_parts = call(
        functools.partial(join_kernel, own_rows), shape(row_count, wide), keep, came_pair, text_back
    )
    image_back = lax.all_to_all(image_parts, IMAGE_GROUP, 0, 0, tiled=True)
    text_grad = call(finish_kernel, unit_shape, text_back, text_unit, text_norm)
    batch = own_rows * math.prod(sizes.values())
    sums = call(functools.partial(stats_kernel, own_rows, batch), shape(8, EXTRA, dtype=F32), image_back)
    sums_came = lax.ppermute(sums, PAIR, swap)
    image_grad = call(finish_kernel, unit_shape, image_back, image_unit, image_norm)
    stats = (sums + sums_came)[0, :3]
    return (image_grad, text_grad, stats)


def solution(mesh):
    img, txt = mesh.shape["img"], mesh.shape["txt"]
    parts = (img // 16, 2, 2, 2, 2, 2, txt // 4, 2)
    split = Mesh(mesh.devices.reshape(parts), IMAGE_ORDER)
    image_spec, text_spec = P(IMAGE_ORDER, None), P(TEXT_ORDER, None)
    return jax.shard_map(
        per_device,
        mesh=split,
        in_specs=(image_spec, text_spec, P(IMAGE_ORDER), P(), P()),
        out_specs=(image_spec, text_spec, P()),
        check_vma=False,
    )
```

```python
import functools
import math
import jax
import jax.numpy as jnp
from jax import lax
from jax.experimental import pallas as pl
from jax.experimental.pallas import tpu as pltpu
from jax.sharding import Mesh, PartitionSpec as P

EPS = 1e-06
EXTRA = 128
F32 = jnp.float32
BF16 = jnp.bfloat16
IMAGE_ORDER = ("z", "xl", "core", "xh", "yh", "y0")
TEXT_ORDER = ("xh", "yh", "y0", "z", "xl", "core")
TEXT_GROUP = ("xh", "xl", "yh")
IMAGE_GROUP = ("z", "y0")
VMEM = pl.BlockSpec(memory_space=pltpu.VMEM)
SMEM = pl.BlockSpec(memory_space=pltpu.SMEM)


def unit_and_norm(rows):
    values = rows.astype(F32)
    norm = jnp.sqrt(jnp.sum(values * values, axis=1, keepdims=True) + EPS)
    return values / norm, norm


def lanes(rows):
    return lax.broadcasted_iota(jnp.int32, (rows, EXTRA), 1)


def pack_image_kernel(image_ref, pair_ref, image_out, image_unit, image_norm):
    rows, width = image_ref.shape
    image_unit[...], image_norm[...] = unit_and_norm(image_ref[...])
    row = lax.broadcasted_iota(jnp.int32, (rows, EXTRA), 0)
    pair = jnp.zeros((rows, EXTRA), jnp.int32)
    for r in range(rows):
        pair = jnp.where(row == r, pair_ref[r], pair)
    lane = lanes(rows)
    high = lax.shift_right_logical(pair, 7)
    low = lax.bitwise_and(pair, 127)
    extra = jnp.where(lane == 0, high, jnp.where(lane == 1, low, 0)).astype(F32)
    image_two = jnp.concatenate([image_unit[...]] * 2, axis=0).astype(BF16)
    extra_two = jnp.concatenate([extra] * 2, axis=0).astype(BF16)
    step = 2 * rows
    for k in range(image_out.shape[0] // step):
        image_out[k * step : (k + 1) * step, :width] = image_two
        image_out[k * step : (k + 1) * step, width:] = extra_two


def pack_text_kernel(text_ref, text_out, text_unit, text_norm):
    text_unit[...], text_norm[...] = unit_and_norm(text_ref[...])
    text_two = jnp.concatenate([text_unit[...]] * 2, axis=0).astype(BF16)
    step = text_two.shape[0]
    for k in range(text_out.shape[0] // step):
        text_out[k * step : (k + 1) * step, :] = text_two


def split_stats(lane, first, values):
    out = jnp.zeros(lane.shape, F32)
    for n, value in enumerate(values):
        high = value.astype(BF16).astype(F32)
        out = jnp.where(lane == first + n, high, out)
        out = jnp.where(lane == first + 3 + n, value - high, out)
    return out


def text_columns(own_rows, sizes, count):
    place = lax.broadcasted_iota(jnp.int32, (1, count), 1)
    peer, row = place // own_rows, place % own_rows
    index = {a: lax.axis_index(a) for a in IMAGE_GROUP + ("core",)}
    for a in reversed(TEXT_GROUP):
        index[a] = peer % sizes[a]
        peer = peer // sizes[a]
    owner = 0
    for a in TEXT_ORDER:
        owner = owner * sizes[a] + index[a]
    return owner * own_rows + row


def stacked(piece_refs, cols):
    return jnp.concatenate([r[:, cols] for r in piece_refs], axis=0)


def scale_of(log_scale_ref):
    return jnp.exp(jnp.zeros((8, 128), F32) + log_scale_ref[0])[0:1, 0:1]


def score_kernel(own_rows, sizes, piece_refs, text_ref, log_scale_ref, bias_ref, text_out, low_out, along_out):
    text = text_ref[...]
    count, width = text.shape
    scale = scale_of(log_scale_ref)
    column = text_columns(own_rows, sizes, count).astype(F32)
    image = stacked(piece_refs, slice(0, width))
    extra = stacked(piece_refs, slice(width, width + EXTRA)).astype(F32)
    pair = extra[:, 0:1] * 128.0 + extra[:, 1:2]
    cosine = lax.dot_general(image, text, (((1,), (1,)), ((), ())), preferred_element_type=F32)
    scaled = scale * cosine
    logits = scaled + bias_ref[0]
    match = pair == column
    arg = jnp.where(match, -logits, logits)
    small = jnp.exp(-jnp.abs(arg))
    inverse = 1.0 / (1.0 + small)
    prob = jnp.where(arg >= 0, inverse, small * inverse)
    dlogit = jnp.where(match, -prob, prob)
    loss = jnp.maximum(arg, 0.0) + jnp.log1p(small)
    low = dlogit.astype(BF16)
    product = low.astype(F32) * scaled
    totals = [jnp.sum(v, axis=(0, 1), keepdims=True) for v in (loss, dlogit, dlogit * scaled)]
    low_out[...] = low
    along_image = jnp.sum(product, axis=1, keepdims=True)
    along_out[...] = jnp.where(lanes(image.shape[0]) == 0, along_image, 0.0)
    along_text = jnp.broadcast_to(jnp.sum(product, axis=0, keepdims=True), (128, count)).T
    along_text = along_text.astype(BF16).astype(F32)
    low_turned = dlogit.T.astype(BF16)
    block = width // 3
    for first in range(0, width, block):
        cols = slice(first, first + block)
        part = scale * jnp.dot(low_turned, image[:, cols], preferred_element_type=F32)
        text_out[:, cols] = (part - along_text[:, 0:1] * text[:, cols].astype(F32)).astype(BF16)
    lane = lanes(count)
    stats = split_stats(lane, 1, [jnp.broadcast_to(t, lane.shape) for t in totals])
    text_out[:, width:] = jnp.where(lane == 0, along_text, stats).astype(BF16)


def image_kernel(piece_refs, text_ref, low_ref, along_ref, log_scale_ref, stay_out, away_out):
    width = text_ref.shape[1]
    scale = scale_of(log_scale_ref)
    half = low_ref.shape[0] // 2
    for target, pieces, rows in (
        (away_out, piece_refs[1:], slice(half, 2 * half)),
        (stay_out, piece_refs[:1], slice(0, half)),
    ):
        low, along = low_ref[rows, :], along_ref[rows, :]
        block = width // 3
        for first in range(0, width, block):
            cols = slice(first, first + block)
            part = scale * jnp.dot(low, text_ref[:, cols], preferred_element_type=F32)
            target[:, cols] = part - along[:, 0:1] * stacked(pieces, cols).astype(F32)
        target[:, width:] = along


def merge_stats(extra, rows):
    peers = extra.shape[0] // rows
    total = jnp.sum(extra.reshape(peers, rows, EXTRA), axis=0)
    return [total[0:1, n : n + 1] + total[0:1, n + 3 : n + 4] for n in (1, 2, 3)]


def join_kernel(own_rows, keep_ref, came_ref, text_back_ref, out_ref):
    width = keep_ref.shape[1] - EXTRA
    out_ref[:, :width] = (keep_ref[:, :width] + came_ref[:, :width]).astype(BF16)
    lane = lanes(keep_ref.shape[0])
    stats = merge_stats(text_back_ref[:, width:].astype(F32), own_rows)
    stats = split_stats(lane, 1, [jnp.broadcast_to(t, lane.shape) for t in stats])
    along = keep_ref[:, width:] + came_ref[:, width:]
    out_ref[:, width:] = jnp.where(lane == 0, along, stats).astype(BF16)


def finish_kernel(parts_ref, unit_ref, norm_ref, grad_out):
    rows, width = unit_ref.shape
    peers = parts_ref.shape[0] // rows
    total = jnp.sum(parts_ref[...].astype(F32).reshape(peers, rows, width + EXTRA), axis=0)
    unit = unit_ref[...]
    grad = total[:, :width] + total[:, width : width + 1] * unit.astype(BF16).astype(F32)
    grad_out[...] = (grad - unit * jnp.sum(unit * grad, axis=1, keepdims=True)) / norm_ref[...]


def stats_kernel(own_rows, batch, parts_ref, out_ref):
    width = parts_ref.shape[1] - EXTRA
    lane = lanes(8)
    out = jnp.zeros(lane.shape, F32)
    for n, value in enumerate(merge_stats(parts_ref[:, width:].astype(F32), own_rows)):
        out = jnp.where(lane == n, value / batch, out)
    out_ref[...] = out


def shape(*dims, dtype=BF16):
    return jax.ShapeDtypeStruct(dims, dtype)


def call(kernel, outs, *args, scalars=0, flops=0, limit=40 * 1024 * 1024):
    size = sum(a.size * a.dtype.itemsize for a in args)
    return pl.pallas_call(
        kernel,
        out_shape=outs,
        in_specs=[VMEM] * (len(args) - scalars) + [SMEM] * scalars,
        out_specs=jax.tree.map(lambda _: VMEM, outs),
        cost_estimate=pl.CostEstimate(flops=flops, bytes_accessed=4 * size, transcendentals=0),
        compiler_params=pltpu.CompilerParams(vmem_limit_bytes=limit),
    )(*args)


def per_device(image_embed, text_embed, pair_index, log_scale, bias):
    own_rows, width = image_embed.shape
    sizes = {a: lax.axis_size(a) for a in IMAGE_ORDER}
    wide = width + EXTRA
    row_count = math.prod(sizes[a] for a in IMAGE_GROUP) * own_rows
    text_count = math.prod(sizes[a] for a in TEXT_GROUP) * own_rows
    unit_shape, norm_shape = shape(own_rows, width, dtype=F32), shape(own_rows, 1, dtype=F32)
    image_send, image_unit, image_norm = call(
        pack_image_kernel, (shape(row_count, wide), unit_shape, norm_shape),
        image_embed, pair_index, scalars=1, limit=None,
    )
    text_send, text_unit, text_norm = call(
        pack_text_kernel, (shape(text_count, width), unit_shape, norm_shape), text_embed, limit=None
    )
    swap = [(0, 1), (1, 0)]
    piece = lax.all_to_all(image_send, IMAGE_GROUP, 0, 0, tiled=True)
    text = lax.all_to_all(text_send, TEXT_GROUP, 0, 0, tiled=True)
    piece_core = lax.ppermute(piece, "core", swap)

    def score(*refs):
        score_kernel(own_rows, sizes, refs[:2], *refs[2:])

    def image_partials(*refs):
        image_kernel(refs[:2], *refs[2:])

    pieces = (piece, piece_core)
    work = 2 * 2 * row_count * text_count * width
    text_parts, low, along = call(
        score,
        (shape(text_count, wide), shape(2 * row_count, text_count), shape(2 * row_count, EXTRA, dtype=F32)),
        *pieces, text, log_scale, bias, scalars=2, flops=2 * work,
    )
    text_back = lax.all_to_all(text_parts, TEXT_GROUP, 0, 0, tiled=True)
    half = shape(row_count, wide, dtype=F32)
    keep, away = call(image_partials, (half, half), *pieces, text, low, along, log_scale, scalars=1, flops=work)
    came = lax.ppermute(away, "core", swap)
    image_parts = call(functools.partial(join_kernel, own_rows), shape(row_count, wide), keep, came, text_back)
    image_back = lax.all_to_all(image_parts, IMAGE_GROUP, 0, 0, tiled=True)
    text_grad = call(finish_kernel, unit_shape, text_back, text_unit, text_norm)
    batch = own_rows * math.prod(sizes.values())
    sums = call(functools.partial(stats_kernel, own_rows, batch), shape(8, EXTRA, dtype=F32), image_back)
    sums_came = lax.ppermute(sums, "core", swap)
    image_grad = call(finish_kernel, unit_shape, image_back, image_unit, image_norm)
    stats = (sums + sums_came)[0, :3]
    return (image_grad, text_grad, stats)


def solution(mesh):
    img, txt = mesh.shape["img"], mesh.shape["txt"]
    parts = (img // 8, 4, 2, 2, txt // 4, 2)
    split = Mesh(mesh.devices.reshape(parts), IMAGE_ORDER)
    image_spec, text_spec = P(IMAGE_ORDER, None), P(TEXT_ORDER, None)
    return jax.shard_map(
        per_device,
        mesh=split,
        in_specs=(image_spec, text_spec, P(IMAGE_ORDER), P(), P()),
        out_specs=(image_spec, text_spec, P()),
        check_vma=False,
    )
```

```python
import functools
import math
import jax
import jax.numpy as jnp
from jax import lax
from jax.experimental import pallas as pl
from jax.experimental.pallas import tpu as pltpu
from jax.sharding import Mesh, PartitionSpec as P

EPS = 1e-06
EXTRA = 128
F32 = jnp.float32
BF16 = jnp.bfloat16
IMAGE_ORDER = ("zh", "z0", "x1", "x0", "core", "xh", "y")
TEXT_ORDER = ("xh", "y", "zh", "z0", "x1", "x0", "core")
TEXT_GROUP = ("y", "zh")
IMAGE_GROUP = ("z0", "xh", "x1")
PAIR = "x0"
VMEM = pl.BlockSpec(memory_space=pltpu.VMEM)
SMEM = pl.BlockSpec(memory_space=pltpu.SMEM)


def unit_and_norm(rows):
    values = rows.astype(F32)
    norm = jnp.sqrt(jnp.sum(values * values, axis=1, keepdims=True) + EPS)
    return values / norm, norm


def lanes(rows):
    return lax.broadcasted_iota(jnp.int32, (rows, EXTRA), 1)


def pack_image_kernel(image_ref, pair_ref, image_out, image_unit, image_norm):
    rows, width = image_ref.shape
    image_unit[...], image_norm[...] = unit_and_norm(image_ref[...])
    row = lax.broadcasted_iota(jnp.int32, (rows, EXTRA), 0)
    pair = jnp.zeros((rows, EXTRA), jnp.int32)
    for r in range(rows):
        pair = jnp.where(row == r, pair_ref[r], pair)
    lane = lanes(rows)
    high = lax.shift_right_logical(pair, 7)
    low = lax.bitwise_and(pair, 127)
    extra = jnp.where(lane == 0, high, jnp.where(lane == 1, low, 0)).astype(F32)
    image_two = jnp.concatenate([image_unit[...]] * 2, axis=0).astype(BF16)
    extra_two = jnp.concatenate([extra] * 2, axis=0).astype(BF16)
    step = 2 * rows
    for k in range(image_out.shape[0] // step):
        image_out[k * step : (k + 1) * step, :width] = image_two
        image_out[k * step : (k + 1) * step, width:] = extra_two


def pack_text_kernel(text_ref, text_out, text_unit, text_norm):
    text_unit[...], text_norm[...] = unit_and_norm(text_ref[...])
    text_two = jnp.concatenate([text_unit[...]] * 2, axis=0).astype(BF16)
    step = text_two.shape[0]
    for k in range(text_out.shape[0] // step):
        text_out[k * step : (k + 1) * step, :] = text_two


def split_stats(lane, first, values):
    out = jnp.zeros(lane.shape, F32)
    for n, value in enumerate(values):
        high = value.astype(BF16).astype(F32)
        out = jnp.where(lane == first + n, high, out)
        out = jnp.where(lane == first + 3 + n, value - high, out)
    return out


def text_columns(own_rows, sizes, count):
    place = lax.broadcasted_iota(jnp.int32, (1, count), 1)
    peer, row = place // own_rows, place % own_rows
    index = {a: lax.axis_index(a) for a in IMAGE_GROUP + (PAIR, "core")}
    for a in reversed(TEXT_GROUP):
        index[a] = peer % sizes[a]
        peer = peer // sizes[a]
    owner = 0
    for a in TEXT_ORDER:
        owner = owner * sizes[a] + index[a]
    return owner * own_rows + row


def stacked(piece_refs, cols):
    return jnp.concatenate([r[:, cols] for r in piece_refs], axis=0)


def scale_of(log_scale_ref):
    return jnp.exp(jnp.zeros((8, 128), F32) + log_scale_ref[0])[0:1, 0:1]


def score_kernel(own_rows, sizes, piece_refs, text_ref, log_scale_ref, bias_ref, text_out, low_out, along_out):
    text = text_ref[...]
    count, width = text.shape
    scale = scale_of(log_scale_ref)
    column = text_columns(own_rows, sizes, count).astype(F32)
    image = stacked(piece_refs, slice(0, width))
    extra = stacked(piece_refs, slice(width, width + EXTRA)).astype(F32)
    pair = extra[:, 0:1] * 128.0 + extra[:, 1:2]
    cosine = lax.dot_general(image, text, (((1,), (1,)), ((), ())), preferred_element_type=F32)
    scaled = scale * cosine
    logits = scaled + bias_ref[0]
    match = pair == column
    arg = jnp.where(match, -logits, logits)
    small = jnp.exp(-jnp.abs(arg))
    inverse = 1.0 / (1.0 + small)
    prob = jnp.where(arg >= 0, inverse, small * inverse)
    dlogit = jnp.where(match, -prob, prob)
    loss = jnp.maximum(arg, 0.0) + jnp.log1p(small)
    low = dlogit.astype(BF16)
    product = low.astype(F32) * scaled
    totals = [jnp.sum(v, axis=(0, 1), keepdims=True) for v in (loss, dlogit, dlogit * scaled)]
    low_out[...] = low
    along_image = jnp.sum(product, axis=1, keepdims=True)
    along_out[...] = jnp.where(lanes(image.shape[0]) == 0, along_image, 0.0)
    along_text = jnp.broadcast_to(jnp.sum(product, axis=0, keepdims=True), (128, count)).T
    along_text = along_text.astype(BF16).astype(F32)
    low_turned = dlogit.T.astype(BF16)
    block = width // 3
    for first in range(0, width, block):
        cols = slice(first, first + block)
        part = scale * jnp.dot(low_turned, image[:, cols], preferred_element_type=F32)
        text_out[:, cols] = (part - along_text[:, 0:1] * text[:, cols].astype(F32)).astype(BF16)
    lane = lanes(count)
    stats = split_stats(lane, 1, [jnp.broadcast_to(t, lane.shape) for t in totals])
    text_out[:, width:] = jnp.where(lane == 0, along_text, stats).astype(BF16)


def image_kernel(piece_refs, text_ref, low_ref, along_ref, log_scale_ref, stay_out, away_out):
    width = text_ref.shape[1]
    scale = scale_of(log_scale_ref)
    half = low_ref.shape[0] // 2
    for target, pieces, rows in (
        (away_out, piece_refs[2:], slice(half, 2 * half)),
        (stay_out, piece_refs[:2], slice(0, half)),
    ):
        low, along = low_ref[rows, :], along_ref[rows, :]
        block = width // 3
        for first in range(0, width, block):
            cols = slice(first, first + block)
            part = scale * jnp.dot(low, text_ref[:, cols], preferred_element_type=F32)
            target[:, cols] = part - along[:, 0:1] * stacked(pieces, cols).astype(F32)
        target[:, width:] = along


def merge_stats(extra, rows):
    peers = extra.shape[0] // rows
    total = jnp.sum(extra.reshape(peers, rows, EXTRA), axis=0)
    return [total[0:1, n : n + 1] + total[0:1, n + 3 : n + 4] for n in (1, 2, 3)]


def add_kernel(stay_ref, came_ref, keep_out, send_out):
    half = keep_out.shape[0]
    keep_out[...] = stay_ref[:half, :] + came_ref[:half, :]
    send_out[...] = (stay_ref[half:, :] + came_ref[half:, :]).astype(BF16)


def join_kernel(own_rows, keep_ref, came_ref, text_back_ref, out_ref):
    width = keep_ref.shape[1] - EXTRA
    out_ref[:, :width] = (keep_ref[:, :width] + came_ref[:, :width].astype(F32)).astype(BF16)
    lane = lanes(keep_ref.shape[0])
    stats = merge_stats(text_back_ref[:, width:].astype(F32), own_rows)
    stats = split_stats(lane, 1, [jnp.broadcast_to(t, lane.shape) for t in stats])
    along = keep_ref[:, width:] + came_ref[:, width:].astype(F32)
    out_ref[:, width:] = jnp.where(lane == 0, along, stats).astype(BF16)


def finish_kernel(parts_ref, unit_ref, norm_ref, grad_out):
    rows, width = unit_ref.shape
    peers = parts_ref.shape[0] // rows
    total = jnp.sum(parts_ref[...].astype(F32).reshape(peers, rows, width + EXTRA), axis=0)
    unit = unit_ref[...]
    grad = total[:, :width] + total[:, width : width + 1] * unit.astype(BF16).astype(F32)
    grad_out[...] = (grad - unit * jnp.sum(unit * grad, axis=1, keepdims=True)) / norm_ref[...]


def stats_kernel(own_rows, batch, parts_ref, out_ref):
    width = parts_ref.shape[1] - EXTRA
    lane = lanes(8)
    out = jnp.zeros(lane.shape, F32)
    for n, value in enumerate(merge_stats(parts_ref[:, width:].astype(F32), own_rows)):
        out = jnp.where(lane == n, value / batch, out)
    out_ref[...] = jnp.broadcast_to(out[None], out_ref.shape)


def shape(*dims, dtype=BF16):
    return jax.ShapeDtypeStruct(dims, dtype)


def call(kernel, outs, *args, scalars=0, flops=0, limit=40 * 1024 * 1024):
    size = sum(a.size * a.dtype.itemsize for a in args)
    return pl.pallas_call(
        kernel,
        out_shape=outs,
        in_specs=[VMEM] * (len(args) - scalars) + [SMEM] * scalars,
        out_specs=jax.tree.map(lambda _: VMEM, outs),
        cost_estimate=pl.CostEstimate(flops=flops, bytes_accessed=4 * size, transcendentals=0),
        compiler_params=pltpu.CompilerParams(vmem_limit_bytes=limit),
    )(*args)


def per_device(image_embed, text_embed, pair_index, log_scale, bias):
    own_rows, width = image_embed.shape
    sizes = {a: lax.axis_size(a) for a in IMAGE_ORDER}
    wide = width + EXTRA
    row_count = math.prod(sizes[a] for a in IMAGE_GROUP) * own_rows
    text_count = math.prod(sizes[a] for a in TEXT_GROUP) * own_rows
    unit_shape, norm_shape = shape(own_rows, width, dtype=F32), shape(own_rows, 1, dtype=F32)
    image_send, image_unit, image_norm = call(
        pack_image_kernel, (shape(row_count, wide), unit_shape, norm_shape),
        image_embed, pair_index, scalars=1, limit=None,
    )
    text_send, text_unit, text_norm = call(
        pack_text_kernel, (shape(text_count, width), unit_shape, norm_shape), text_embed, limit=None
    )
    piece = lax.all_to_all(image_send, IMAGE_GROUP, 0, 0, tiled=True)
    text = lax.all_to_all(text_send, TEXT_GROUP, 0, 0, tiled=True)
    swap = [(0, 1), (1, 0)]
    piece_pair = lax.ppermute(piece, PAIR, swap)
    piece_core = lax.ppermute(piece, "core", swap)
    piece_both = lax.ppermute(piece_pair, "core", swap)

    def score(a, b, c, d, *rest):
        score_kernel(own_rows, sizes, (a, b, c, d), *rest)

    def image_partials(a, b, c, d, *rest):
        image_kernel((a, b, c, d), *rest)

    pieces = (piece, piece_pair, piece_core, piece_both)
    work = 2 * 4 * row_count * text_count * width
    text_parts, low, along = call(
        score,
        (shape(text_count, wide), shape(4 * row_count, text_count), shape(4 * row_count, EXTRA, dtype=F32)),
        *pieces, text, log_scale, bias, scalars=2, flops=2 * work,
    )
    text_back = lax.all_to_all(text_parts, TEXT_GROUP, 0, 0, tiled=True)
    half = shape(2 * row_count, wide, dtype=F32)
    stay, away = call(image_partials, (half, half), *pieces, text, low, along, log_scale, scalars=1, flops=work)
    came = lax.ppermute(away, "core", swap)
    keep, send = call(
        add_kernel, (shape(row_count, wide, dtype=F32), shape(row_count, wide)), stay, came
    )
    came_pair = lax.ppermute(send, PAIR, swap)
    image_parts = call(
        functools.partial(join_kernel, own_rows), shape(row_count, wide), keep, came_pair, text_back
    )
    image_back = lax.all_to_all(image_parts, IMAGE_GROUP, 0, 0, tiled=True)
    text_grad = call(finish_kernel, unit_shape, text_back, text_unit, text_norm)
    four = sizes[PAIR] * sizes["core"]
    batch = own_rows * math.prod(sizes.values())
    sums = call(functools.partial(stats_kernel, own_rows, batch), shape(four, 8, EXTRA, dtype=F32), image_back)
    sums = lax.all_to_all(sums, (PAIR, "core"), 0, 0, tiled=True)
    image_grad = call(finish_kernel, unit_shape, image_back, image_unit, image_norm)
    stats = jnp.sum(sums[:, 0, :3], axis=0)
    return (image_grad, text_grad, stats)


def solution(mesh):
    img, txt = mesh.shape["img"], mesh.shape["txt"]
    parts = (img // 16, 2, 2, 2, 2, 2, txt // 2)
    split = Mesh(mesh.devices.reshape(parts), IMAGE_ORDER)
    image_spec, text_spec = P(IMAGE_ORDER, None), P(TEXT_ORDER, None)
    return jax.shard_map(
        per_device,
        mesh=split,
        in_specs=(image_spec, text_spec, P(IMAGE_ORDER), P(), P()),
        out_specs=(image_spec, text_spec, P()),
        check_vma=False,
    )
```

```python
import functools
import math
import jax
import jax.numpy as jnp
from jax import lax
from jax.experimental import pallas as pl
from jax.experimental.pallas import tpu as pltpu
from jax.sharding import Mesh, PartitionSpec as P

EPS = 1e-06
EXTRA = 128
F32 = jnp.float32
BF16 = jnp.bfloat16
IMAGE_ORDER = ("zh", "zl", "xl", "core", "xh", "yh", "y0")
TEXT_ORDER = ("xh", "yh", "y0", "zh", "zl", "xl", "core")
TEXT_GROUP = ("xh", "xl", "yh")
IMAGE_GROUP = ("zl", "y0")
PAIR = "zh"
VMEM = pl.BlockSpec(memory_space=pltpu.VMEM)
SMEM = pl.BlockSpec(memory_space=pltpu.SMEM)


def unit_and_norm(rows):
    values = rows.astype(F32)
    norm = jnp.sqrt(jnp.sum(values * values, axis=1, keepdims=True) + EPS)
    return values / norm, norm


def lanes(rows):
    return lax.broadcasted_iota(jnp.int32, (rows, EXTRA), 1)


def pack_image_kernel(image_ref, pair_ref, image_out, image_unit, image_norm):
    rows, width = image_ref.shape
    image_unit[...], image_norm[...] = unit_and_norm(image_ref[...])
    row = lax.broadcasted_iota(jnp.int32, (rows, EXTRA), 0)
    pair = jnp.zeros((rows, EXTRA), jnp.int32)
    for r in range(rows):
        pair = jnp.where(row == r, pair_ref[r], pair)
    lane = lanes(rows)
    high = lax.shift_right_logical(pair, 7)
    low = lax.bitwise_and(pair, 127)
    extra = jnp.where(lane == 0, high, jnp.where(lane == 1, low, 0)).astype(F32)
    image_two = jnp.concatenate([image_unit[...]] * 2, axis=0).astype(BF16)
    extra_two = jnp.concatenate([extra] * 2, axis=0).astype(BF16)
    step = 2 * rows
    for k in range(image_out.shape[0] // step):
        image_out[k * step : (k + 1) * step, :width] = image_two
        image_out[k * step : (k + 1) * step, width:] = extra_two


def pack_text_kernel(text_ref, text_out, text_unit, text_norm):
    text_unit[...], text_norm[...] = unit_and_norm(text_ref[...])
    text_two = jnp.concatenate([text_unit[...]] * 2, axis=0).astype(BF16)
    step = text_two.shape[0]
    for k in range(text_out.shape[0] // step):
        text_out[k * step : (k + 1) * step, :] = text_two


def split_stats(lane, first, values):
    out = jnp.zeros(lane.shape, F32)
    for n, value in enumerate(values):
        high = value.astype(BF16).astype(F32)
        out = jnp.where(lane == first + n, high, out)
        out = jnp.where(lane == first + 3 + n, value - high, out)
    return out


def text_columns(own_rows, sizes, count):
    place = lax.broadcasted_iota(jnp.int32, (1, count), 1)
    peer, row = place // own_rows, place % own_rows
    index = {a: lax.axis_index(a) for a in IMAGE_GROUP + (PAIR, "core")}
    for a in reversed(TEXT_GROUP):
        index[a] = peer % sizes[a]
        peer = peer // sizes[a]
    owner = 0
    for a in TEXT_ORDER:
        owner = owner * sizes[a] + index[a]
    return owner * own_rows + row


def stacked(piece_refs, cols):
    return jnp.concatenate([r[:, cols] for r in piece_refs], axis=0)


def scale_of(log_scale_ref):
    return jnp.exp(jnp.zeros((8, 128), F32) + log_scale_ref[0])[0:1, 0:1]


def score_kernel(own_rows, sizes, piece_refs, text_ref, log_scale_ref, bias_ref, text_out, low_out, along_out):
    text = text_ref[...]
    count, width = text.shape
    scale = scale_of(log_scale_ref)
    column = text_columns(own_rows, sizes, count).astype(F32)
    image = stacked(piece_refs, slice(0, width))
    extra = stacked(piece_refs, slice(width, width + EXTRA)).astype(F32)
    pair = extra[:, 0:1] * 128.0 + extra[:, 1:2]
    cosine = lax.dot_general(image, text, (((1,), (1,)), ((), ())), preferred_element_type=F32)
    scaled = scale * cosine
    logits = scaled + bias_ref[0]
    match = pair == column
    arg = jnp.where(match, -logits, logits)
    small = jnp.exp(-jnp.abs(arg))
    inverse = 1.0 / (1.0 + small)
    prob = jnp.where(arg >= 0, inverse, small * inverse)
    dlogit = jnp.where(match, -prob, prob)
    loss = jnp.maximum(arg, 0.0) + jnp.log1p(small)
    low = dlogit.astype(BF16)
    product = low.astype(F32) * scaled
    totals = [jnp.sum(v, axis=(0, 1), keepdims=True) for v in (loss, dlogit, dlogit * scaled)]
    low_out[...] = low
    along_image = jnp.sum(product, axis=1, keepdims=True)
    along_out[...] = jnp.where(lanes(image.shape[0]) == 0, along_image, 0.0)
    along_text = jnp.broadcast_to(jnp.sum(product, axis=0, keepdims=True), (128, count)).T
    along_text = along_text.astype(BF16).astype(F32)
    low_turned = dlogit.T.astype(BF16)
    block = width // 3
    for first in range(0, width, block):
        cols = slice(first, first + block)
        part = scale * jnp.dot(low_turned, image[:, cols], preferred_element_type=F32)
        text_out[:, cols] = (part - along_text[:, 0:1] * text[:, cols].astype(F32)).astype(BF16)
    lane = lanes(count)
    stats = split_stats(lane, 1, [jnp.broadcast_to(t, lane.shape) for t in totals])
    text_out[:, width:] = jnp.where(lane == 0, along_text, stats).astype(BF16)


def image_kernel(piece_refs, text_ref, low_ref, along_ref, log_scale_ref, stay_out, away_out):
    width = text_ref.shape[1]
    scale = scale_of(log_scale_ref)
    half = low_ref.shape[0] // 2
    for target, pieces, rows in (
        (away_out, piece_refs[2:], slice(half, 2 * half)),
        (stay_out, piece_refs[:2], slice(0, half)),
    ):
        low, along = low_ref[rows, :], along_ref[rows, :]
        block = width // 3
        for first in range(0, width, block):
            cols = slice(first, first + block)
            part = scale * jnp.dot(low, text_ref[:, cols], preferred_element_type=F32)
            target[:, cols] = part - along[:, 0:1] * stacked(pieces, cols).astype(F32)
        target[:, width:] = along


def merge_stats(extra, rows):
    peers = extra.shape[0] // rows
    total = jnp.sum(extra.reshape(peers, rows, EXTRA), axis=0)
    return [total[0:1, n : n + 1] + total[0:1, n + 3 : n + 4] for n in (1, 2, 3)]


def add_kernel(stay_ref, came_ref, keep_out, send_out):
    half = keep_out.shape[0]
    keep_out[...] = stay_ref[:half, :] + came_ref[:half, :]
    send_out[...] = (stay_ref[half:, :] + came_ref[half:, :]).astype(BF16)


def join_kernel(own_rows, keep_ref, came_ref, text_back_ref, out_ref):
    width = keep_ref.shape[1] - EXTRA
    out_ref[:, :width] = (keep_ref[:, :width] + came_ref[:, :width].astype(F32)).astype(BF16)
    lane = lanes(keep_ref.shape[0])
    stats = merge_stats(text_back_ref[:, width:].astype(F32), own_rows)
    stats = split_stats(lane, 1, [jnp.broadcast_to(t, lane.shape) for t in stats])
    along = keep_ref[:, width:] + came_ref[:, width:].astype(F32)
    out_ref[:, width:] = jnp.where(lane == 0, along, stats).astype(BF16)


def finish_kernel(parts_ref, unit_ref, norm_ref, grad_out):
    rows, width = unit_ref.shape
    peers = parts_ref.shape[0] // rows
    total = jnp.sum(parts_ref[...].astype(F32).reshape(peers, rows, width + EXTRA), axis=0)
    unit = unit_ref[...]
    grad = total[:, :width] + total[:, width : width + 1] * unit.astype(BF16).astype(F32)
    grad_out[...] = (grad - unit * jnp.sum(unit * grad, axis=1, keepdims=True)) / norm_ref[...]


def stats_kernel(own_rows, batch, parts_ref, out_ref):
    width = parts_ref.shape[1] - EXTRA
    lane = lanes(8)
    out = jnp.zeros(lane.shape, F32)
    for n, value in enumerate(merge_stats(parts_ref[:, width:].astype(F32), own_rows)):
        out = jnp.where(lane == n, value / batch, out)
    out_ref[...] = jnp.broadcast_to(out[None], out_ref.shape)


def shape(*dims, dtype=BF16):
    return jax.ShapeDtypeStruct(dims, dtype)


def call(kernel, outs, *args, scalars=0, flops=0, limit=40 * 1024 * 1024):
    size = sum(a.size * a.dtype.itemsize for a in args)
    return pl.pallas_call(
        kernel,
        out_shape=outs,
        in_specs=[VMEM] * (len(args) - scalars) + [SMEM] * scalars,
        out_specs=jax.tree.map(lambda _: VMEM, outs),
        cost_estimate=pl.CostEstimate(flops=flops, bytes_accessed=4 * size, transcendentals=0),
        compiler_params=pltpu.CompilerParams(vmem_limit_bytes=limit),
    )(*args)


def per_device(image_embed, text_embed, pair_index, log_scale, bias):
    own_rows, width = image_embed.shape
    sizes = {a: lax.axis_size(a) for a in IMAGE_ORDER}
    wide = width + EXTRA
    row_count = math.prod(sizes[a] for a in IMAGE_GROUP) * own_rows
    text_count = math.prod(sizes[a] for a in TEXT_GROUP) * own_rows
    unit_shape, norm_shape = shape(own_rows, width, dtype=F32), shape(own_rows, 1, dtype=F32)
    image_send, image_unit, image_norm = call(
        pack_image_kernel, (shape(row_count, wide), unit_shape, norm_shape),
        image_embed, pair_index, scalars=1, limit=None,
    )
    text_send, text_unit, text_norm = call(
        pack_text_kernel, (shape(text_count, width), unit_shape, norm_shape), text_embed, limit=None
    )
    piece = lax.all_to_all(image_send, IMAGE_GROUP, 0, 0, tiled=True)
    text = lax.all_to_all(text_send, TEXT_GROUP, 0, 0, tiled=True)
    swap = [(0, 1), (1, 0)]
    piece_pair = lax.ppermute(piece, PAIR, swap)
    piece_core = lax.ppermute(piece, "core", swap)
    piece_both = lax.ppermute(piece_pair, "core", swap)

    def score(a, b, c, d, *rest):
        score_kernel(own_rows, sizes, (a, b, c, d), *rest)

    def image_partials(a, b, c, d, *rest):
        image_kernel((a, b, c, d), *rest)

    pieces = (piece, piece_pair, piece_core, piece_both)
    work = 2 * 4 * row_count * text_count * width
    text_parts, low, along = call(
        score,
        (shape(text_count, wide), shape(4 * row_count, text_count), shape(4 * row_count, EXTRA, dtype=F32)),
        *pieces, text, log_scale, bias, scalars=2, flops=2 * work,
    )
    text_back = lax.all_to_all(text_parts, TEXT_GROUP, 0, 0, tiled=True)
    half = shape(2 * row_count, wide, dtype=F32)
    stay, away = call(image_partials, (half, half), *pieces, text, low, along, log_scale, scalars=1, flops=work)
    came = lax.ppermute(away, "core", swap)
    keep, send = call(
        add_kernel, (shape(row_count, wide, dtype=F32), shape(row_count, wide)), stay, came
    )
    came_pair = lax.ppermute(send, PAIR, swap)
    image_parts = call(
        functools.partial(join_kernel, own_rows), shape(row_count, wide), keep, came_pair, text_back
    )
    image_back = lax.all_to_all(image_parts, IMAGE_GROUP, 0, 0, tiled=True)
    text_grad = call(finish_kernel, unit_shape, text_back, text_unit, text_norm)
    four = sizes[PAIR] * sizes["core"]
    batch = own_rows * math.prod(sizes.values())
    sums = call(functools.partial(stats_kernel, own_rows, batch), shape(four, 8, EXTRA, dtype=F32), image_back)
    sums = lax.all_to_all(sums, (PAIR, "core"), 0, 0, tiled=True)
    image_grad = call(finish_kernel, unit_shape, image_back, image_unit, image_norm)
    stats = jnp.sum(sums[:, 0, :3], axis=0)
    return (image_grad, text_grad, stats)


def solution(mesh):
    img, txt = mesh.shape["img"], mesh.shape["txt"]
    parts = (2, img // 16, 4, 2, 2, txt // 4, 2)
    split = Mesh(mesh.devices.reshape(parts), IMAGE_ORDER)
    image_spec, text_spec = P(IMAGE_ORDER, None), P(TEXT_ORDER, None)
    return jax.shard_map(
        per_device,
        mesh=split,
        in_specs=(image_spec, text_spec, P(IMAGE_ORDER), P(), P()),
        out_specs=(image_spec, text_spec, P()),
        check_vma=False,
    )
```

```python
import functools
import math
import jax
import jax.numpy as jnp
from jax import lax
from jax.experimental import pallas as pl
from jax.experimental.pallas import tpu as pltpu
from jax.sharding import Mesh, PartitionSpec as P

EPS = 1e-06
EXTRA = 128
F32 = jnp.float32
BF16 = jnp.bfloat16
IMAGE_ORDER = ("zh", "z0", "xl", "core", "xh", "yh", "y0")
TEXT_ORDER = ("xh", "yh", "y0", "zh", "z0", "xl", "core")
TEXT_GROUP = ("xh", "xl", "yh")
IMAGE_GROUP = ("zh", "y0")
PAIR = "z0"
VMEM = pl.BlockSpec(memory_space=pltpu.VMEM)
SMEM = pl.BlockSpec(memory_space=pltpu.SMEM)


def unit_and_norm(rows):
    values = rows.astype(F32)
    norm = jnp.sqrt(jnp.sum(values * values, axis=1, keepdims=True) + EPS)
    return values / norm, norm


def lanes(rows):
    return lax.broadcasted_iota(jnp.int32, (rows, EXTRA), 1)


def pack_image_kernel(image_ref, pair_ref, image_out, image_unit, image_norm):
    rows, width = image_ref.shape
    image_unit[...], image_norm[...] = unit_and_norm(image_ref[...])
    row = lax.broadcasted_iota(jnp.int32, (rows, EXTRA), 0)
    pair = jnp.zeros((rows, EXTRA), jnp.int32)
    for r in range(rows):
        pair = jnp.where(row == r, pair_ref[r], pair)
    lane = lanes(rows)
    high = lax.shift_right_logical(pair, 7)
    low = lax.bitwise_and(pair, 127)
    extra = jnp.where(lane == 0, high, jnp.where(lane == 1, low, 0)).astype(F32)
    image_two = jnp.concatenate([image_unit[...]] * 2, axis=0).astype(BF16)
    extra_two = jnp.concatenate([extra] * 2, axis=0).astype(BF16)
    step = 2 * rows
    for k in range(image_out.shape[0] // step):
        image_out[k * step : (k + 1) * step, :width] = image_two
        image_out[k * step : (k + 1) * step, width:] = extra_two


def pack_text_kernel(text_ref, text_out, text_unit, text_norm):
    text_unit[...], text_norm[...] = unit_and_norm(text_ref[...])
    text_two = jnp.concatenate([text_unit[...]] * 2, axis=0).astype(BF16)
    step = text_two.shape[0]
    for k in range(text_out.shape[0] // step):
        text_out[k * step : (k + 1) * step, :] = text_two


def split_stats(lane, first, values):
    out = jnp.zeros(lane.shape, F32)
    for n, value in enumerate(values):
        high = value.astype(BF16).astype(F32)
        out = jnp.where(lane == first + n, high, out)
        out = jnp.where(lane == first + 3 + n, value - high, out)
    return out


def text_columns(own_rows, sizes, count):
    place = lax.broadcasted_iota(jnp.int32, (1, count), 1)
    peer, row = place // own_rows, place % own_rows
    index = {a: lax.axis_index(a) for a in IMAGE_GROUP + (PAIR, "core")}
    for a in reversed(TEXT_GROUP):
        index[a] = peer % sizes[a]
        peer = peer // sizes[a]
    owner = 0
    for a in TEXT_ORDER:
        owner = owner * sizes[a] + index[a]
    return owner * own_rows + row


def stacked(piece_refs, cols):
    return jnp.concatenate([r[:, cols] for r in piece_refs], axis=0)


def scale_of(log_scale_ref):
    return jnp.exp(jnp.zeros((8, 128), F32) + log_scale_ref[0])[0:1, 0:1]


def score_kernel(own_rows, sizes, piece_refs, text_ref, log_scale_ref, bias_ref, text_out, low_out, along_out, text_made, sems):
    copies = []

    def send(cols):
        copies.append(pltpu.make_async_copy(text_made.at[:, cols], text_out.at[:, cols], sems.at[len(copies)]))
        copies[-1].start()

    text = text_ref[...]
    count, width = text.shape
    scale = scale_of(log_scale_ref)
    column = text_columns(own_rows, sizes, count).astype(F32)
    image = stacked(piece_refs, slice(0, width))
    extra = stacked(piece_refs, slice(width, width + EXTRA)).astype(F32)
    pair = extra[:, 0:1] * 128.0 + extra[:, 1:2]
    cosine = lax.dot_general(image, text, (((1,), (1,)), ((), ())), preferred_element_type=F32)
    scaled = scale * cosine
    logits = scaled + bias_ref[0]
    match = pair == column
    arg = jnp.where(match, -logits, logits)
    small = jnp.exp(-jnp.abs(arg))
    inverse = 1.0 / (1.0 + small)
    prob = jnp.where(arg >= 0, inverse, small * inverse)
    dlogit = jnp.where(match, -prob, prob)
    loss = jnp.maximum(arg, 0.0) + jnp.log1p(small)
    low = dlogit.astype(BF16)
    product = low.astype(F32) * scaled
    totals = [jnp.sum(v, axis=(0, 1), keepdims=True) for v in (loss, dlogit, dlogit * scaled)]
    low_out[...] = low
    along_image = jnp.sum(product, axis=1, keepdims=True)
    along_out[...] = jnp.where(lanes(image.shape[0]) == 0, along_image, 0.0)
    along_text = jnp.broadcast_to(jnp.sum(product, axis=0, keepdims=True), (128, count)).T
    along_text = along_text.astype(BF16).astype(F32)
    low_turned = dlogit.T.astype(BF16)
    lane = lanes(count)
    stats = split_stats(lane, 1, [jnp.broadcast_to(t, lane.shape) for t in totals])
    text_made[:, width:] = jnp.where(lane == 0, along_text, stats).astype(BF16)
    send(slice(width, width + EXTRA))
    block = width // 3
    for first in range(0, width, block):
        cols = slice(first, first + block)
        part = scale * jnp.dot(low_turned, image[:, cols], preferred_element_type=F32)
        text_made[:, cols] = (part - along_text[:, 0:1] * text[:, cols].astype(F32)).astype(BF16)
        send(cols)
    for copy in copies:
        copy.wait()


def image_kernel(piece_refs, text_ref, low_ref, along_ref, log_scale_ref, stay_out, away_out):
    width = text_ref.shape[1]
    scale = scale_of(log_scale_ref)
    half = low_ref.shape[0] // 2
    for target, pieces, rows in (
        (away_out, piece_refs[2:], slice(half, 2 * half)),
        (stay_out, piece_refs[:2], slice(0, half)),
    ):
        low, along = low_ref[rows, :], along_ref[rows, :]
        block = width // 3
        for first in range(0, width, block):
            cols = slice(first, first + block)
            part = scale * jnp.dot(low, text_ref[:, cols], preferred_element_type=F32)
            target[:, cols] = part - along[:, 0:1] * stacked(pieces, cols).astype(F32)
        target[:, width:] = along


def merge_stats(extra, rows):
    peers = extra.shape[0] // rows
    total = jnp.sum(extra.reshape(peers, rows, EXTRA), axis=0)
    return [total[0:1, n : n + 1] + total[0:1, n + 3 : n + 4] for n in (1, 2, 3)]


def add_kernel(stay_ref, came_ref, keep_out, send_out):
    half = keep_out.shape[0]
    keep_out[...] = stay_ref[:half, :] + came_ref[:half, :]
    send_out[...] = (stay_ref[half:, :] + came_ref[half:, :]).astype(BF16)


def join_kernel(own_rows, keep_ref, came_ref, text_back_ref, out_ref):
    width = keep_ref.shape[1] - EXTRA
    out_ref[:, :width] = (keep_ref[:, :width] + came_ref[:, :width].astype(F32)).astype(BF16)
    lane = lanes(keep_ref.shape[0])
    stats = merge_stats(text_back_ref[:, width:].astype(F32), own_rows)
    stats = split_stats(lane, 1, [jnp.broadcast_to(t, lane.shape) for t in stats])
    along = keep_ref[:, width:] + came_ref[:, width:].astype(F32)
    out_ref[:, width:] = jnp.where(lane == 0, along, stats).astype(BF16)


def finish_kernel(parts_ref, unit_ref, norm_ref, grad_out):
    rows, width = unit_ref.shape
    peers = parts_ref.shape[0] // rows
    total = jnp.sum(parts_ref[...].astype(F32).reshape(peers, rows, width + EXTRA), axis=0)
    unit = unit_ref[...]
    grad = total[:, :width] + total[:, width : width + 1] * unit.astype(BF16).astype(F32)
    grad_out[...] = (grad - unit * jnp.sum(unit * grad, axis=1, keepdims=True)) / norm_ref[...]


def stats_kernel(own_rows, batch, parts_ref, out_ref):
    width = parts_ref.shape[1] - EXTRA
    lane = lanes(8)
    out = jnp.zeros(lane.shape, F32)
    for n, value in enumerate(merge_stats(parts_ref[:, width:].astype(F32), own_rows)):
        out = jnp.where(lane == n, value / batch, out)
    out_ref[...] = jnp.broadcast_to(out[None], out_ref.shape)


def shape(*dims, dtype=BF16):
    return jax.ShapeDtypeStruct(dims, dtype)


def call(kernel, outs, *args, scalars=0, flops=0, limit=40 * 1024 * 1024, out_specs=None, scratch=()):
    size = sum(a.size * a.dtype.itemsize for a in args)
    return pl.pallas_call(
        kernel,
        out_shape=outs,
        in_specs=[VMEM] * (len(args) - scalars) + [SMEM] * scalars,
        out_specs=out_specs or jax.tree.map(lambda _: VMEM, outs),
        scratch_shapes=list(scratch),
        cost_estimate=pl.CostEstimate(flops=flops, bytes_accessed=4 * size, transcendentals=0),
        compiler_params=pltpu.CompilerParams(vmem_limit_bytes=limit),
    )(*args)


def per_device(image_embed, text_embed, pair_index, log_scale, bias):
    own_rows, width = image_embed.shape
    sizes = {a: lax.axis_size(a) for a in IMAGE_ORDER}
    wide = width + EXTRA
    row_count = math.prod(sizes[a] for a in IMAGE_GROUP) * own_rows
    text_count = math.prod(sizes[a] for a in TEXT_GROUP) * own_rows
    unit_shape, norm_shape = shape(own_rows, width, dtype=F32), shape(own_rows, 1, dtype=F32)
    image_send, image_unit, image_norm = call(
        pack_image_kernel, (shape(row_count, wide), unit_shape, norm_shape),
        image_embed, pair_index, scalars=1, limit=None,
    )
    text_send, text_unit, text_norm = call(
        pack_text_kernel, (shape(text_count, width), unit_shape, norm_shape), text_embed, limit=None
    )
    piece = lax.all_to_all(image_send, IMAGE_GROUP, 0, 0, tiled=True)
    text = lax.all_to_all(text_send, TEXT_GROUP, 0, 0, tiled=True)
    swap = [(0, 1), (1, 0)]
    piece_pair = lax.ppermute(piece, PAIR, swap)
    piece_core = lax.ppermute(piece, "core", swap)
    piece_both = lax.ppermute(piece_pair, "core", swap)

    def score(a, b, c, d, *rest):
        score_kernel(own_rows, sizes, (a, b, c, d), *rest)

    def image_partials(a, b, c, d, *rest):
        image_kernel((a, b, c, d), *rest)

    pieces = (piece, piece_pair, piece_core, piece_both)
    work = 2 * 4 * row_count * text_count * width
    text_parts, low, along = call(
        score,
        (shape(text_count, wide), shape(4 * row_count, text_count), shape(4 * row_count, EXTRA, dtype=F32)),
        *pieces, text, log_scale, bias, scalars=2, flops=2 * work,
        out_specs=(pl.BlockSpec(memory_space=pl.ANY), VMEM, VMEM),
        scratch=[pltpu.VMEM((text_count, wide), BF16), pltpu.SemaphoreType.DMA((4,))],
    )
    text_back = lax.all_to_all(text_parts, TEXT_GROUP, 0, 0, tiled=True)
    half = shape(2 * row_count, wide, dtype=F32)
    stay, away = call(image_partials, (half, half), *pieces, text, low, along, log_scale, scalars=1, flops=work)
    came = lax.ppermute(away, "core", swap)
    keep, send = call(
        add_kernel, (shape(row_count, wide, dtype=F32), shape(row_count, wide)), stay, came
    )
    came_pair = lax.ppermute(send, PAIR, swap)
    image_parts = call(
        functools.partial(join_kernel, own_rows), shape(row_count, wide), keep, came_pair, text_back
    )
    image_back = lax.all_to_all(image_parts, IMAGE_GROUP, 0, 0, tiled=True)
    text_grad = call(finish_kernel, unit_shape, text_back, text_unit, text_norm)
    four = sizes[PAIR] * sizes["core"]
    batch = own_rows * math.prod(sizes.values())
    sums = call(functools.partial(stats_kernel, own_rows, batch), shape(four, 8, EXTRA, dtype=F32), image_back)
    sums = lax.all_to_all(sums, (PAIR, "core"), 0, 0, tiled=True)
    image_grad = call(finish_kernel, unit_shape, image_back, image_unit, image_norm)
    stats = jnp.sum(sums[:, 0, :3], axis=0)
    return (image_grad, text_grad, stats)


def solution(mesh):
    img, txt = mesh.shape["img"], mesh.shape["txt"]
    parts = (img // 16, 2, 4, 2, 2, txt // 4, 2)
    split = Mesh(mesh.devices.reshape(parts), IMAGE_ORDER)
    image_spec, text_spec = P(IMAGE_ORDER, None), P(TEXT_ORDER, None)
    return jax.shard_map(
        per_device,
        mesh=split,
        in_specs=(image_spec, text_spec, P(IMAGE_ORDER), P(), P()),
        out_specs=(image_spec, text_spec, P()),
        check_vma=False,
    )
```

```python
import functools
import math
import jax
import jax.numpy as jnp
from jax import lax
from jax.experimental import pallas as pl
from jax.experimental.pallas import tpu as pltpu
from jax.sharding import Mesh, PartitionSpec as P

EPS = 1e-06
EXTRA = 128
F32 = jnp.float32
BF16 = jnp.bfloat16
IMAGE_ORDER = ("zh", "z0", "xl", "core", "xh", "yh", "y0")
TEXT_ORDER = ("xh", "yh", "y0", "zh", "z0", "xl", "core")
TEXT_GROUP = ("xh", "xl", "zh")
IMAGE_GROUP = ("z0", "yh")
PAIR = "y0"
VMEM = pl.BlockSpec(memory_space=pltpu.VMEM)
SMEM = pl.BlockSpec(memory_space=pltpu.SMEM)


def unit_and_norm(rows):
    values = rows.astype(F32)
    norm = jnp.sqrt(jnp.sum(values * values, axis=1, keepdims=True) + EPS)
    return values / norm, norm


def lanes(rows):
    return lax.broadcasted_iota(jnp.int32, (rows, EXTRA), 1)


def pack_kernel(image_ref, text_ref, pair_ref, image_out, text_out, image_unit, image_norm, text_unit, text_norm):
    rows, width = image_ref.shape
    image_unit[...], image_norm[...] = unit_and_norm(image_ref[...])
    text_unit[...], text_norm[...] = unit_and_norm(text_ref[...])
    row = lax.broadcasted_iota(jnp.int32, (rows, EXTRA), 0)
    pair = jnp.zeros((rows, EXTRA), jnp.int32)
    for r in range(rows):
        pair = jnp.where(row == r, pair_ref[r], pair)
    lane = lanes(rows)
    high = lax.shift_right_logical(pair, 7)
    low = lax.bitwise_and(pair, 127)
    extra = jnp.where(lane == 0, high, jnp.where(lane == 1, low, 0)).astype(F32)
    image_two = jnp.concatenate([image_unit[...]] * 2, axis=0).astype(BF16)
    text_two = jnp.concatenate([text_unit[...]] * 2, axis=0).astype(BF16)
    extra_two = jnp.concatenate([extra] * 2, axis=0).astype(BF16)
    step = 2 * rows
    for k in range(image_out.shape[0] // step):
        image_out[k * step : (k + 1) * step, :width] = image_two
        image_out[k * step : (k + 1) * step, width:] = extra_two
    for k in range(text_out.shape[0] // step):
        text_out[k * step : (k + 1) * step, :] = text_two


def split_stats(lane, first, values):
    out = jnp.zeros(lane.shape, F32)
    for n, value in enumerate(values):
        high = value.astype(BF16).astype(F32)
        out = jnp.where(lane == first + n, high, out)
        out = jnp.where(lane == first + 3 + n, value - high, out)
    return out


def text_columns(own_rows, sizes, count):
    place = lax.broadcasted_iota(jnp.int32, (1, count), 1)
    peer, row = place // own_rows, place % own_rows
    index = {a: lax.axis_index(a) for a in IMAGE_GROUP + (PAIR, "core")}
    for a in reversed(TEXT_GROUP):
        index[a] = peer % sizes[a]
        peer = peer // sizes[a]
    owner = 0
    for a in TEXT_ORDER:
        owner = owner * sizes[a] + index[a]
    return owner * own_rows + row


def score_kernel(own_rows, sizes, piece_refs, text_ref, log_scale_ref, bias_ref, text_out, stay_out, away_out):
    text = text_ref[...]
    count, width = text.shape
    scale = jnp.exp(jnp.zeros((8, 128), F32) + log_scale_ref[0])[0:1, 0:1]
    column = text_columns(own_rows, sizes, count).astype(F32)
    image = jnp.concatenate([r[:, :width] for r in piece_refs], axis=0)
    extra = jnp.concatenate([r[:, width:] for r in piece_refs], axis=0).astype(F32)
    pair = extra[:, 0:1] * 128.0 + extra[:, 1:2]
    cosine = lax.dot_general(image, text, (((1,), (1,)), ((), ())), preferred_element_type=F32)
    scaled = scale * cosine
    logits = scaled + bias_ref[0]
    match = pair == column
    arg = jnp.where(match, -logits, logits)
    small = jnp.exp(-jnp.abs(arg))
    inverse = 1.0 / (1.0 + small)
    prob = jnp.where(arg >= 0, inverse, small * inverse)
    dlogit = jnp.where(match, -prob, prob)
    loss = jnp.maximum(arg, 0.0) + jnp.log1p(small)
    low = dlogit.astype(BF16)
    product = low.astype(F32) * scaled
    totals = [jnp.sum(v, axis=(0, 1), keepdims=True) for v in (loss, dlogit, dlogit * scaled)]
    along_image = jnp.sum(product, axis=1, keepdims=True)
    along_text = jnp.broadcast_to(jnp.sum(product, axis=0, keepdims=True), (128, count)).T
    along_text = along_text.astype(BF16).astype(F32)
    low_turned = dlogit.T.astype(BF16)
    half = image.shape[0] // 2
    block = width // 3
    for first in range(0, width, block):
        cols = slice(first, first + block)
        part = scale * jnp.dot(low, text[:, cols], preferred_element_type=F32)
        part = part - along_image * image[:, cols].astype(F32)
        stay_out[:, cols] = part[:half]
        away_out[:, cols] = part[half:]
        part = scale * jnp.dot(low_turned, image[:, cols], preferred_element_type=F32)
        text_out[:, cols] = (part - along_text[:, 0:1] * text[:, cols].astype(F32)).astype(BF16)
    kept = jnp.where(lanes(2 * half) == 0, along_image, 0.0)
    stay_out[:, width:] = kept[:half]
    away_out[:, width:] = kept[half:]
    lane = lanes(count)
    stats = split_stats(lane, 1, [jnp.broadcast_to(t, lane.shape) for t in totals])
    text_out[:, width:] = jnp.where(lane == 0, along_text, stats).astype(BF16)


def merge_stats(extra, rows):
    peers = extra.shape[0] // rows
    total = jnp.sum(extra.reshape(peers, rows, EXTRA), axis=0)
    return [total[0:1, n : n + 1] + total[0:1, n + 3 : n + 4] for n in (1, 2, 3)]


def add_kernel(stay_ref, came_ref, keep_out, send_out):
    half = keep_out.shape[0]
    keep_out[...] = stay_ref[:half, :] + came_ref[:half, :]
    send_out[...] = stay_ref[half:, :] + came_ref[half:, :]


def join_kernel(own_rows, keep_ref, came_ref, text_back_ref, out_ref):
    width = keep_ref.shape[1] - EXTRA
    out_ref[:, :width] = (keep_ref[:, :width] + came_ref[:, :width]).astype(BF16)
    lane = lanes(keep_ref.shape[0])
    stats = merge_stats(text_back_ref[:, width:].astype(F32), own_rows)
    stats = split_stats(lane, 1, [jnp.broadcast_to(t, lane.shape) for t in stats])
    along = keep_ref[:, width:] + came_ref[:, width:]
    out_ref[:, width:] = jnp.where(lane == 0, along, stats).astype(BF16)


def finish_kernel(parts_ref, unit_ref, norm_ref, grad_out):
    rows, width = unit_ref.shape
    peers = parts_ref.shape[0] // rows
    total = jnp.sum(parts_ref[...].astype(F32).reshape(peers, rows, width + EXTRA), axis=0)
    unit = unit_ref[...]
    grad = total[:, :width] + total[:, width : width + 1] * unit.astype(BF16).astype(F32)
    grad_out[...] = (grad - unit * jnp.sum(unit * grad, axis=1, keepdims=True)) / norm_ref[...]


def stats_kernel(own_rows, parts_ref, out_ref):
    width = parts_ref.shape[1] - EXTRA
    lane = lanes(8)
    out = jnp.zeros(lane.shape, F32)
    for n, value in enumerate(merge_stats(parts_ref[:, width:].astype(F32), own_rows)):
        out = jnp.where(lane == n, value, out)
    out_ref[...] = jnp.broadcast_to(out[None], out_ref.shape)


def shape(*dims, dtype=BF16):
    return jax.ShapeDtypeStruct(dims, dtype)


def call(kernel, outs, *args, scalars=0, flops=0, limit=40 * 1024 * 1024):
    size = sum(a.size * a.dtype.itemsize for a in args)
    return pl.pallas_call(
        kernel,
        out_shape=outs,
        in_specs=[VMEM] * (len(args) - scalars) + [SMEM] * scalars,
        out_specs=jax.tree.map(lambda _: VMEM, outs),
        cost_estimate=pl.CostEstimate(flops=flops, bytes_accessed=4 * size, transcendentals=0),
        compiler_params=pltpu.CompilerParams(vmem_limit_bytes=limit),
    )(*args)


def per_device(image_embed, text_embed, pair_index, log_scale, bias):
    own_rows, width = image_embed.shape
    sizes = {a: lax.axis_size(a) for a in IMAGE_ORDER}
    wide = width + EXTRA
    row_count = math.prod(sizes[a] for a in IMAGE_GROUP) * own_rows
    text_count = math.prod(sizes[a] for a in TEXT_GROUP) * own_rows
    unit_shape, norm_shape = shape(own_rows, width, dtype=F32), shape(own_rows, 1, dtype=F32)
    image_send, text_send, image_unit, image_norm, text_unit, text_norm = call(
        pack_kernel,
        (shape(row_count, wide), shape(text_count, width), unit_shape, norm_shape, unit_shape, norm_shape),
        image_embed, text_embed, pair_index, scalars=1, limit=None,
    )
    swap = [(0, 1), (1, 0)]
    piece = lax.all_to_all(image_send, IMAGE_GROUP, 0, 0, tiled=True)
    text = lax.all_to_all(text_send, TEXT_GROUP, 0, 0, tiled=True)
    piece_pair = lax.ppermute(piece, PAIR, swap)
    piece_core = lax.ppermute(piece, "core", swap)
    piece_both = lax.ppermute(piece_pair, "core", swap)

    def score(a, b, c, d, text_ref, *rest):
        score_kernel(own_rows, sizes, (a, b, c, d), text_ref, *rest)

    text_parts, stay, away = call(
        score,
        (shape(text_count, wide), shape(2 * row_count, wide, dtype=F32), shape(2 * row_count, wide, dtype=F32)),
        piece, piece_pair, piece_core, piece_both, text, log_scale, bias,
        scalars=2, flops=3 * 2 * 4 * row_count * text_count * width,
    )
    text_back = lax.all_to_all(text_parts, TEXT_GROUP, 0, 0, tiled=True)
    came = lax.ppermute(away, "core", swap)
    quarter = shape(row_count, wide, dtype=F32)
    keep, send = call(add_kernel, (quarter, quarter), stay, came)
    came_pair = lax.ppermute(send, PAIR, swap)
    image_parts = call(
        functools.partial(join_kernel, own_rows), shape(row_count, wide), keep, came_pair, text_back
    )
    image_back = lax.all_to_all(image_parts, IMAGE_GROUP, 0, 0, tiled=True)
    text_grad = call(finish_kernel, unit_shape, text_back, text_unit, text_norm)
    four = sizes[PAIR] * sizes["core"]
    sums = call(functools.partial(stats_kernel, own_rows), shape(four, 8, EXTRA, dtype=F32), image_back)
    sums = lax.all_to_all(sums, (PAIR, "core"), 0, 0, tiled=True)
    image_grad = call(finish_kernel, unit_shape, image_back, image_unit, image_norm)
    batch = own_rows * math.prod(sizes.values())
    stats = jnp.sum(sums[:, 0, :3], axis=0) / batch
    return (image_grad, text_grad, stats)


def solution(mesh):
    img, txt = mesh.shape["img"], mesh.shape["txt"]
    parts = (img // 16, 2, 4, 2, 2, txt // 4, 2)
    split = Mesh(mesh.devices.reshape(parts), IMAGE_ORDER)
    image_spec, text_spec = P(IMAGE_ORDER, None), P(TEXT_ORDER, None)
    return jax.shard_map(
        per_device,
        mesh=split,
        in_specs=(image_spec, text_spec, P(IMAGE_ORDER), P(), P()),
        out_specs=(image_spec, text_spec, P()),
        check_vma=False,
    )
```

```python
import functools
import math
import jax
import jax.numpy as jnp
from jax import lax
from jax.experimental import pallas as pl
from jax.experimental.pallas import tpu as pltpu
from jax.sharding import Mesh, PartitionSpec as P

EPS = 1e-06
EXTRA = 128
F32 = jnp.float32
BF16 = jnp.bfloat16
IMAGE_ORDER = ("zh", "z0", "xl", "core", "xh", "yh", "y0")
TEXT_ORDER = ("xh", "yh", "y0", "zh", "z0", "xl", "core")
TEXT_GROUP = ("xh", "xl", "yh")
IMAGE_GROUP = ("zh", "y0")
PAIR = "z0"
VMEM = pl.BlockSpec(memory_space=pltpu.VMEM)
SMEM = pl.BlockSpec(memory_space=pltpu.SMEM)


def unit_and_norm(rows):
    values = rows.astype(F32)
    norm = jnp.sqrt(jnp.sum(values * values, axis=1, keepdims=True) + EPS)
    return values / norm, norm


def lanes(rows):
    return lax.broadcasted_iota(jnp.int32, (rows, EXTRA), 1)


def pack_kernel(image_ref, text_ref, pair_ref, image_out, text_out, image_unit, image_norm, text_unit, text_norm):
    rows, width = image_ref.shape
    image_unit[...], image_norm[...] = unit_and_norm(image_ref[...])
    text_unit[...], text_norm[...] = unit_and_norm(text_ref[...])
    row = lax.broadcasted_iota(jnp.int32, (rows, EXTRA), 0)
    pair = jnp.zeros((rows, EXTRA), jnp.int32)
    for r in range(rows):
        pair = jnp.where(row == r, pair_ref[r], pair)
    lane = lanes(rows)
    high = lax.shift_right_logical(pair, 7)
    low = lax.bitwise_and(pair, 127)
    extra = jnp.where(lane == 0, high, jnp.where(lane == 1, low, 0)).astype(F32)
    image_two = jnp.concatenate([image_unit[...]] * 2, axis=0).astype(BF16)
    text_two = jnp.concatenate([text_unit[...]] * 2, axis=0).astype(BF16)
    extra_two = jnp.concatenate([extra] * 2, axis=0).astype(BF16)
    step = 2 * rows
    for k in range(image_out.shape[0] // step):
        image_out[k * step : (k + 1) * step, :width] = image_two
        image_out[k * step : (k + 1) * step, width:] = extra_two
    for k in range(text_out.shape[0] // step):
        text_out[k * step : (k + 1) * step, :] = text_two


def split_stats(lane, first, values):
    out = jnp.zeros(lane.shape, F32)
    for n, value in enumerate(values):
        high = value.astype(BF16).astype(F32)
        out = jnp.where(lane == first + n, high, out)
        out = jnp.where(lane == first + 3 + n, value - high, out)
    return out


def text_columns(own_rows, sizes, count):
    place = lax.broadcasted_iota(jnp.int32, (1, count), 1)
    peer, row = place // own_rows, place % own_rows
    index = {a: lax.axis_index(a) for a in IMAGE_GROUP + (PAIR, "core")}
    for a in reversed(TEXT_GROUP):
        index[a] = peer % sizes[a]
        peer = peer // sizes[a]
    owner = 0
    for a in TEXT_ORDER:
        owner = owner * sizes[a] + index[a]
    return owner * own_rows + row


def score_kernel(own_rows, sizes, piece_refs, text_ref, log_scale_ref, bias_ref, text_out, stay_out, away_out):
    text = text_ref[...]
    count, width = text.shape
    scale = jnp.exp(jnp.zeros((8, 128), F32) + log_scale_ref[0])[0:1, 0:1]
    column = text_columns(own_rows, sizes, count).astype(F32)
    image = jnp.concatenate([r[:, :width] for r in piece_refs], axis=0)
    extra = jnp.concatenate([r[:, width:] for r in piece_refs], axis=0).astype(F32)
    pair = extra[:, 0:1] * 128.0 + extra[:, 1:2]
    cosine = lax.dot_general(image, text, (((1,), (1,)), ((), ())), preferred_element_type=F32)
    scaled = scale * cosine
    logits = scaled + bias_ref[0]
    match = pair == column
    arg = jnp.where(match, -logits, logits)
    small = jnp.exp(-jnp.abs(arg))
    inverse = 1.0 / (1.0 + small)
    prob = jnp.where(arg >= 0, inverse, small * inverse)
    dlogit = jnp.where(match, -prob, prob)
    loss = jnp.maximum(arg, 0.0) + jnp.log1p(small)
    low = dlogit.astype(BF16)
    product = low.astype(F32) * scaled
    totals = [jnp.sum(v, axis=(0, 1), keepdims=True) for v in (loss, dlogit, dlogit * scaled)]
    along_image = jnp.sum(product, axis=1, keepdims=True)
    along_text = jnp.broadcast_to(jnp.sum(product, axis=0, keepdims=True), (128, count)).T
    along_text = along_text.astype(BF16).astype(F32)
    low_turned = dlogit.T.astype(BF16)
    half = image.shape[0] // 2
    block = width // 3
    for first in range(0, width, block):
        cols = slice(first, first + block)
        part = scale * jnp.dot(low, text[:, cols], preferred_element_type=F32)
        part = part - along_image * image[:, cols].astype(F32)
        stay_out[:, cols] = part[:half]
        away_out[:, cols] = part[half:]
        part = scale * jnp.dot(low_turned, image[:, cols], preferred_element_type=F32)
        text_out[:, cols] = (part - along_text[:, 0:1] * text[:, cols].astype(F32)).astype(BF16)
    kept = jnp.where(lanes(2 * half) == 0, along_image, 0.0)
    stay_out[:, width:] = kept[:half]
    away_out[:, width:] = kept[half:]
    lane = lanes(count)
    stats = split_stats(lane, 1, [jnp.broadcast_to(t, lane.shape) for t in totals])
    text_out[:, width:] = jnp.where(lane == 0, along_text, stats).astype(BF16)


def merge_stats(extra, rows):
    peers = extra.shape[0] // rows
    total = jnp.sum(extra.reshape(peers, rows, EXTRA), axis=0)
    return [total[0:1, n : n + 1] + total[0:1, n + 3 : n + 4] for n in (1, 2, 3)]


def add_kernel(stay_ref, came_ref, keep_out, send_out):
    half = keep_out.shape[0]
    keep_out[...] = stay_ref[:half, :] + came_ref[:half, :]
    send_out[...] = stay_ref[half:, :] + came_ref[half:, :]


def join_kernel(own_rows, keep_ref, came_ref, text_back_ref, out_ref):
    width = keep_ref.shape[1] - EXTRA
    out_ref[:, :width] = (keep_ref[:, :width] + came_ref[:, :width]).astype(BF16)
    lane = lanes(keep_ref.shape[0])
    stats = merge_stats(text_back_ref[:, width:].astype(F32), own_rows)
    stats = split_stats(lane, 1, [jnp.broadcast_to(t, lane.shape) for t in stats])
    along = keep_ref[:, width:] + came_ref[:, width:]
    out_ref[:, width:] = jnp.where(lane == 0, along, stats).astype(BF16)


def finish_kernel(parts_ref, unit_ref, norm_ref, grad_out):
    rows, width = unit_ref.shape
    peers = parts_ref.shape[0] // rows
    total = jnp.sum(parts_ref[...].astype(F32).reshape(peers, rows, width + EXTRA), axis=0)
    unit = unit_ref[...]
    grad = total[:, :width] + total[:, width : width + 1] * unit.astype(BF16).astype(F32)
    grad_out[...] = (grad - unit * jnp.sum(unit * grad, axis=1, keepdims=True)) / norm_ref[...]


def stats_kernel(own_rows, batch, parts_ref, out_ref):
    width = parts_ref.shape[1] - EXTRA
    lane = lanes(8)
    out = jnp.zeros(lane.shape, F32)
    for n, value in enumerate(merge_stats(parts_ref[:, width:].astype(F32), own_rows)):
        out = jnp.where(lane == n, value / batch, out)
    out_ref[...] = out


def shape(*dims, dtype=BF16):
    return jax.ShapeDtypeStruct(dims, dtype)


def call(kernel, outs, *args, scalars=0, flops=0, limit=40 * 1024 * 1024):
    size = sum(a.size * a.dtype.itemsize for a in args)
    return pl.pallas_call(
        kernel,
        out_shape=outs,
        in_specs=[VMEM] * (len(args) - scalars) + [SMEM] * scalars,
        out_specs=jax.tree.map(lambda _: VMEM, outs),
        cost_estimate=pl.CostEstimate(flops=flops, bytes_accessed=4 * size, transcendentals=0),
        compiler_params=pltpu.CompilerParams(vmem_limit_bytes=limit),
    )(*args)


def per_device(image_embed, text_embed, pair_index, log_scale, bias):
    own_rows, width = image_embed.shape
    sizes = {a: lax.axis_size(a) for a in IMAGE_ORDER}
    wide = width + EXTRA
    row_count = math.prod(sizes[a] for a in IMAGE_GROUP) * own_rows
    text_count = math.prod(sizes[a] for a in TEXT_GROUP) * own_rows
    unit_shape, norm_shape = shape(own_rows, width, dtype=F32), shape(own_rows, 1, dtype=F32)
    image_send, text_send, image_unit, image_norm, text_unit, text_norm = call(
        pack_kernel,
        (shape(row_count, wide), shape(text_count, width), unit_shape, norm_shape, unit_shape, norm_shape),
        image_embed, text_embed, pair_index, scalars=1, limit=None,
    )
    swap = [(0, 1), (1, 0)]
    piece = lax.all_to_all(image_send, IMAGE_GROUP, 0, 0, tiled=True)
    text = lax.all_to_all(text_send, TEXT_GROUP, 0, 0, tiled=True)
    piece_pair = lax.ppermute(piece, PAIR, swap)
    piece_core = lax.ppermute(piece, "core", swap)
    piece_both = lax.ppermute(piece_pair, "core", swap)

    def score(a, b, c, d, text_ref, *rest):
        score_kernel(own_rows, sizes, (a, b, c, d), text_ref, *rest)

    text_parts, stay, away = call(
        score,
        (shape(text_count, wide), shape(2 * row_count, wide, dtype=F32), shape(2 * row_count, wide, dtype=F32)),
        piece, piece_pair, piece_core, piece_both, text, log_scale, bias,
        scalars=2, flops=3 * 2 * 4 * row_count * text_count * width,
    )
    text_back = lax.all_to_all(text_parts, TEXT_GROUP, 0, 0, tiled=True)
    came = lax.ppermute(away, "core", swap)
    quarter = shape(row_count, wide, dtype=F32)
    keep, send = call(add_kernel, (quarter, quarter), stay, came)
    came_pair = lax.ppermute(send, PAIR, swap)
    image_parts = call(
        functools.partial(join_kernel, own_rows), shape(row_count, wide), keep, came_pair, text_back
    )
    image_back = lax.all_to_all(image_parts, IMAGE_GROUP, 0, 0, tiled=True)
    text_grad = call(finish_kernel, unit_shape, text_back, text_unit, text_norm)
    batch = own_rows * math.prod(sizes.values())
    sums = call(functools.partial(stats_kernel, own_rows, batch), shape(8, EXTRA, dtype=F32), image_back)
    others = (
        lax.ppermute(sums, "core", swap),
        lax.ppermute(sums, PAIR, swap),
        lax.ppermute(sums, (PAIR, "core"), [(0, 3), (1, 2), (2, 1), (3, 0)]),
    )
    image_grad = call(finish_kernel, unit_shape, image_back, image_unit, image_norm)
    stats = ((sums + others[0]) + (others[1] + others[2]))[0, :3]
    return (image_grad, text_grad, stats)


def solution(mesh):
    img, txt = mesh.shape["img"], mesh.shape["txt"]
    parts = (img // 16, 2, 4, 2, 2, txt // 4, 2)
    split = Mesh(mesh.devices.reshape(parts), IMAGE_ORDER)
    image_spec, text_spec = P(IMAGE_ORDER, None), P(TEXT_ORDER, None)
    return jax.shard_map(
        per_device,
        mesh=split,
        in_specs=(image_spec, text_spec, P(IMAGE_ORDER), P(), P()),
        out_specs=(image_spec, text_spec, P()),
        check_vma=False,
    )
```
